32 devices in a mesh: lat: 8 (over y, x, core), lon: 4 (over z).
Axes of the slice: x: 2, y: 2, z: 4, core: 2. Of those that a mesh axis runs over, the one named last changes fastest.
Arguments:
- latent: bfloat16 [16, 5760, 256], P('lon', 'lat'), may hold values from -6 to 6
- psi_one: bfloat16 [16, 9, 5, 5], P('lon'), may hold values from -4 to 4
- psi_two: bfloat16 [16, 9, 5, 5], P('lon'), may hold values from -4 to 4
- cycle_one: float32 [16, 9, 2, 4], P('lon'), may hold values from -4 to 4
- cycle_two: float32 [16, 9, 2, 4], P('lon'), may hold values from -4 to 4
- w_one: bfloat16 [2304, 256], replicated, may hold values from -0.125 to 0.125
- w_two: bfloat16 [2304, 256], replicated, may hold values from -0.125 to 0.125
- b_one: float32 [256], replicated, may hold values from -3 to 3
- b_two: float32 [256], replicated, may hold values from -3 to 3
- lon_start: int32 [16], replicated, may hold values from -2 to 0, as said below
- lon_width: int32 [16], replicated, may hold values from 1 to 5
- polar_counts: int32 [2], replicated, may hold values from 1 to 4, as said below
Outputs:
- result: bfloat16 [16, 5760, 256], P('lon', 'lat')
The draws below stay inside these ranges and needn't reach their ends.
Inputs may be any that keep to these rules, and one draw needn't show every extreme that they name: lon_start[i] + lon_width[i] - 1 <= 2 in every row. `polar_counts`: at least one of the two counts is exactly 4.
All inputs are finite; a program needn't handle non-finite values.
Results may differ from the reference program's by a relative error of at most 0.005.
Values may be sent and summed in bfloat16 or wider, within the bound.
No kernel may reach another device: no remote copies, remote signals or barrier semaphores. Data moves between devices by JAX's collectives and lax.ppermute only.
A program may use at most 256 MiB of HBM per device.

```python
import math
import jax
import jax.numpy as jnp
from jax import lax

ROWS_DEV = 4
C = 256
K = 9
HARM = 4
TAPS = 5
NLAT = 16
NLON = 5760


def support_pair(key):
    inner = jax.random.fold_in(key, 11)
    first_key, second_key = jax.random.split(inner)
    start_cols = jax.random.randint(first_key, (NLAT,), -2, 1)
    spread = jax.random.randint(second_key, (NLAT,), 0, 1 << 20)
    width_cols = 1 + spread % (3 - start_cols)
    start_cols = start_cols.at[0].set(-2).at[1].set(0)
    width_cols = width_cols.at[0].set(5).at[1].set(1)
    return (start_cols.astype(jnp.int32), width_cols.astype(jnp.int32))


def draw_lon_start(key, part):
    return support_pair(key)[0]


def draw_lon_width(key, part):
    return support_pair(key)[1]


def draw_polar_counts(key, part):
    first_key, second_key = jax.random.split(jax.random.fold_in(key, 5))
    which_pole = jax.random.randint(first_key, (), 0, 2)
    other_count = jax.random.randint(second_key, (), 1, ROWS_DEV + 1)
    full_count = jnp.int32(ROWS_DEV)
    north_first = jnp.stack([full_count, other_count.astype(jnp.int32)])
    south_first = jnp.stack([other_count.astype(jnp.int32), full_count])
    return jnp.where(which_pole == 0, north_first, south_first).astype(jnp.int32)


def block_levels(rng, shape, pieces, least, top_value):
    loudness = 1.0
    for position, shards_of in pieces:
        draws = jax.random.uniform(jax.random.fold_in(jax.random.fold_in(rng, 6), position), (shards_of,), jnp.float32, least / len(pieces), top_value / len(pieces))
        loudness = loudness * jnp.repeat(jnp.exp(draws), shape[position] // shards_of).reshape((-1,) + (1,) * (len(shape) - 1 - position))
    return loudness


def gaussian(rng, extent, deviation, reach, shards=(), kind=jnp.bfloat16):
    values = deviation * jax.random.normal(rng, extent, jnp.float32)
    if shards:
        values = values * block_levels(rng, extent, shards, -0.22, 0.18)
    return jnp.clip(values, -reach, reach).astype(kind)


def setup_inputs(seed: int = 0) -> dict:
    keys = jax.random.split(jax.random.key(seed), 13)
    latent = gaussian(keys[0], (NLAT, NLON, C), 1.0, 6.0, ((0, 4), (1, 8)))
    psi_one = gaussian(keys[1], (NLAT, K, TAPS, TAPS), 0.3, 4.0, ((0, 4),))
    psi_two = gaussian(keys[2], (NLAT, K, TAPS, TAPS), 0.3, 4.0, ((0, 4),))
    cycle_one = gaussian(keys[3], (NLAT, K, 2, HARM), 0.3, 4.0, ((0, 4),), jnp.float32)
    cycle_two = gaussian(keys[4], (NLAT, K, 2, HARM), 0.3, 4.0, ((0, 4),), jnp.float32)
    w_one = gaussian(keys[5], (K * C, C), (K * C) ** -0.5, 0.125)
    w_two = gaussian(keys[6], (K * C, C), (K * C) ** -0.5, 0.125)
    b_one = gaussian(keys[7], (C,), 0.5, 3.0, (), jnp.float32)
    b_two = gaussian(keys[8], (C,), 0.5, 3.0, (), jnp.float32)
    lon_start = draw_lon_start(jax.random.fold_in(keys[12], 71), 0)
    lon_width = draw_lon_width(jax.random.fold_in(keys[12], 71), 0)
    polar_counts = draw_polar_counts(jax.random.fold_in(keys[12], 71), 0)
    return {"latent": latent, "psi_one": psi_one, "psi_two": psi_two, "cycle_one": cycle_one, "cycle_two": cycle_two, "w_one": w_one, "w_two": w_two, "b_one": b_one, "b_two": b_two, "lon_start": lon_start, "lon_width": lon_width, "polar_counts": polar_counts}


def cycle_tables(columns, cycle_length, count):
    orders = jnp.arange(count, dtype=jnp.int32)
    phase_index = ((columns[:, None] % cycle_length) * orders[None, :]) % cycle_length
    angles = phase_index.astype(jnp.float32) * jnp.float32(2.0 * math.pi / cycle_length)
    return jnp.cos(angles), jnp.sin(angles)


def tap_weights(psi, lon_start, lon_width):
    offsets = jnp.arange(5, dtype=jnp.int32)
    shifted = lon_start[:, None, None] + offsets[None, :, None]
    target = offsets[None, None, :] - 2
    select = ((shifted == target) & (offsets[None, :, None] < lon_width[:, None, None])).astype(jnp.float32)
    mixed_taps = jnp.einsum("ikrq,iqd->ikrd", psi.astype(jnp.float32), select, precision=lax.Precision.HIGHEST)
    return mixed_taps.astype(jnp.bfloat16).reshape(psi.shape[0], psi.shape[1], 25)


def harmonics(source, cos_low, sin_low, cycle_length):
    norm_factor = cycle_length ** -0.5
    cos_part = jnp.einsum("jm,ijc->imc", cos_low.astype(jnp.float32), source.astype(jnp.float32), precision=lax.Precision.HIGHEST) * norm_factor
    sin_part = jnp.einsum("jm,ijc->imc", sin_low.astype(jnp.float32), source.astype(jnp.float32), precision=lax.Precision.HIGHEST) * norm_factor
    return cos_part, sin_part


def convolve(padded, tap_rows, coef_rows, polar_mask, cos_part, sin_part, cos_full, sin_full, kernel, bias_row):
    col_count = cos_full.shape[0]
    basis_count = tap_rows.shape[1]
    channels = padded.shape[2]
    kernel_cube = kernel.reshape(basis_count, channels, kernel.shape[1]).astype(jnp.float32)

    def one_row(row_items):
        row_index, tap_row, coef_row, polar_row, cos_row, sin_row = row_items
        row_band = lax.dynamic_slice_in_dim(padded, row_index, 5, 0).astype(jnp.float32)
        tap_stack = jnp.stack([row_band[r, d:d + col_count] for r in range(5) for d in range(5)])
        near_sum = jnp.einsum("kt,tjc->kjc", tap_row.astype(jnp.float32), tap_stack, precision=lax.Precision.HIGHEST)
        cycle_term = jnp.einsum("kmc,jm->kjc", coef_row[:, 0, :, None] * cos_row[None], cos_full, precision=lax.Precision.HIGHEST)
        cycle_term = cycle_term + jnp.einsum("kmc,jm->kjc", coef_row[:, 1, :, None] * sin_row[None], sin_full, precision=lax.Precision.HIGHEST)
        feature = lax.optimization_barrier((near_sum + polar_row * cycle_term).astype(jnp.bfloat16)).astype(jnp.float32)
        return jnp.einsum("kjc,kco->jo", feature, kernel_cube, precision=lax.Precision.HIGHEST)

    row_numbers = jnp.arange(tap_rows.shape[0], dtype=jnp.int32)
    produced = lax.map(one_row, (row_numbers, tap_rows, coef_rows, polar_mask, cos_part, sin_part))
    return produced + bias_row


def reference(latent, psi_one, psi_two, cycle_one, cycle_two, w_one, w_two, b_one, b_two, lon_start, lon_width, polar_counts):
    row_global = jnp.arange(NLAT, dtype=jnp.int32)
    polar_mask = ((row_global < polar_counts[0]) | (row_global >= NLAT - polar_counts[1])).astype(jnp.float32)
    columns = jnp.arange(NLON, dtype=jnp.int32)
    cos_full, sin_full = cycle_tables(columns, NLON, HARM)
    cos_low = cos_full.astype(jnp.bfloat16)
    sin_low = sin_full.astype(jnp.bfloat16)

    def with_margins(source):
        wrapped = jnp.concatenate([source[:, -2:], source, source[:, :2]], axis=1)
        return jnp.pad(wrapped, ((2, 2), (0, 0), (0, 0)))

    def layer(source, psi, coef, kernel, bias_row):
        tap_rows = tap_weights(psi, lon_start, lon_width)
        cos_part, sin_part = harmonics(source, cos_low, sin_low, NLON)
        return convolve(with_margins(source), tap_rows, coef, polar_mask, cos_part, sin_part, cos_full, sin_full, kernel, bias_row)

    hidden = jax.nn.gelu(layer(latent, psi_one, cycle_one, w_one, b_one), approximate=False).astype(jnp.bfloat16)
    return layer(hidden, psi_two, cycle_two, w_two, b_two).astype(jnp.bfloat16)
```

```python
import functools
import math

import jax
import jax.numpy as jnp
from jax import lax
from jax.experimental import pallas as pl
from jax.experimental.pallas import tpu as pltpu
from jax.sharding import PartitionSpec as P

BLOCK = 16
GROUP = 6
HALO = 16
TAPS = 5
VMEM_BYTES = 40 * 1024 * 1024


def vmem_params():
    return pltpu.CompilerParams(vmem_limit_bytes=VMEM_BYTES)


def shift_pairs(axis, periodic):
    count = lax.axis_size(axis)
    forward = [(i, i + 1) for i in range(count - 1)]
    if periodic:
        forward.append((count - 1, 0))
    return forward, [(target, source) for source, target in forward]


def tap_weights(psi, lon_start, lon_width):
    offsets = jnp.arange(TAPS, dtype=jnp.int32)
    shifted = lon_start[:, None, None] + offsets[None, :, None]
    target = offsets[None, None, :] - 2
    select = ((shifted == target) & (offsets[None, :, None] < lon_width[:, None, None])).astype(
        jnp.float32
    )
    mixed_taps = jnp.einsum(
        "ikrq,iqd->ikrd", psi.astype(jnp.float32), select, precision=lax.Precision.HIGHEST
    )
    return mixed_taps.astype(jnp.bfloat16)


def tap_matrix(psi, lon_start, lon_width, first):
    rows, basis = psi.shape[0], psi.shape[1]
    taps = tap_weights(psi, lon_start, lon_width)
    spread = jnp.stack(
        [jnp.pad(taps[i], ((0, 0), (i, rows - 1 - i), (0, 0))) for i in range(rows)], axis=1
    )
    height = rows + TAPS - 1
    spread = spread.reshape(basis * rows, height * TAPS)
    shape = (height, TAPS, BLOCK, 2, height, BLOCK)
    it = lambda axis: lax.broadcasted_iota(jnp.int32, shape, axis)
    place = (it(0) == it(4)) & (it(3) * BLOCK + it(5) == first + it(2) + it(1))
    place = place.astype(jnp.bfloat16).reshape(height * TAPS, BLOCK * 2 * height * BLOCK)
    matrix = jnp.dot(spread, place, preferred_element_type=jnp.float32).astype(jnp.bfloat16)
    return matrix.reshape(basis * rows * BLOCK, 2 * height * BLOCK)


def wave_rows(columns, cycle_length, count):
    orders = jnp.arange(count, dtype=jnp.int32)
    phase_index = columns[None, :] % cycle_length * orders[:, None] % cycle_length
    angles = phase_index.astype(jnp.float32) * jnp.float32(2.0 * math.pi / cycle_length)
    return jnp.concatenate([jnp.cos(angles), jnp.sin(angles)], axis=0)


def wave_table(waves, rows):
    high = waves.astype(jnp.bfloat16)
    low = (waves - high.astype(jnp.float32)).astype(jnp.bfloat16)
    lanes = jnp.concatenate([high, low, high, jnp.zeros_like(high)], axis=0)
    blocks = waves.shape[1] // BLOCK
    lanes = lanes.T.reshape(blocks, 1, BLOCK, 1, lanes.shape[0])
    own = jnp.eye(rows, dtype=jnp.bfloat16).reshape(1, rows, 1, rows, 1)
    return (lanes * own).reshape(blocks * rows * BLOCK, rows * lanes.shape[-1])


def cycle_kernel(norm_factor, parts_ref, coef_ref, polar_ref, w_ref, out_ref):
    total = parts_ref[0]
    for p in range(1, parts_ref.shape[0]):
        total = total + parts_ref[p]
    total = total * norm_factor
    channels = total.shape[1]
    acc = jnp.zeros((2 * total.shape[0], w_ref.shape[1]), jnp.float32)
    for k in range(coef_ref.shape[1]):
        term = total * coef_ref[:, k : k + 1]
        high = term.astype(jnp.bfloat16)
        low = (term - high.astype(jnp.float32)).astype(jnp.bfloat16)
        acc += jnp.dot(
            jnp.concatenate([high, low], axis=0),
            w_ref[k * channels : (k + 1) * channels],
            preferred_element_type=jnp.float32,
        )
    mixed = (acc[: total.shape[0]] + acc[total.shape[0] :]) * polar_ref[:, 0:1]
    high = mixed.astype(jnp.bfloat16).astype(jnp.float32)
    low = mixed - high
    pieces = []
    for i in range(total.shape[0] // 8):
        own = slice(8 * i, 8 * i + 8)
        pieces += [high[own], high[own], low[own], jnp.zeros_like(low[own])]
    out_ref[...] = jnp.concatenate(pieces, axis=0).astype(jnp.bfloat16)


def conv_kernel(blocks, first_block, gelu, blocked, *refs):
    up_ref, mid_ref, low_ref, dn_ref, taps_ref, w_ref, bias_ref, waves_ref, cycle_ref = refs[:9]
    refs = refs[9:]
    if gelu:
        own_ref, top_ref, bot_ref, harm_ref, feat_ref = refs
        harm_ref[...] = jnp.zeros_like(harm_ref)
    else:
        out_ref, feat_ref = refs
    channels = w_ref.shape[1]
    basis = w_ref.shape[0] // channels
    slab = 4 * BLOCK

    def half(b):
        if blocked:
            parts = [up_ref[b], mid_ref[b], low_ref[b], dn_ref[b]]
        else:
            at = pl.ds(pl.multiple_of(b * BLOCK, BLOCK), BLOCK)
            own = pl.ds(pl.multiple_of((b + first_block) * BLOCK, BLOCK), BLOCK)
            parts = [up_ref[:, at], mid_ref[:, own], dn_ref[:, at]]
        return jnp.concatenate(parts, axis=0).reshape(8 * BLOCK, channels)

    def group(start, count):
        for t in range(count):
            window = jnp.concatenate([half(start + t), half(start + t + 1)], axis=0)
            feature = jnp.dot(taps_ref[...], window, preferred_element_type=jnp.float32)
            feature = feature.astype(jnp.bfloat16)
            for k in range(basis):
                feat_ref[t * slab : (t + 1) * slab, k * channels : (k + 1) * channels] = feature[
                    k * slab : (k + 1) * slab
                ]
        rows = pl.ds(pl.multiple_of(start * slab, slab), count * slab)
        mixed = jnp.dot(
            feat_ref[: count * slab], w_ref[...], preferred_element_type=jnp.float32
        )
        mixed += jnp.dot(waves_ref[rows], cycle_ref[...], preferred_element_type=jnp.float32)
        mixed += bias_ref[...]
        if gelu:
            mixed = 0.5 * mixed * (1.0 + lax.erf(mixed * math.sqrt(0.5)))
        value = mixed.astype(jnp.bfloat16)
        for t in range(count):
            piece = value[t * slab : (t + 1) * slab].reshape(4, BLOCK, channels)
            if gelu:
                top_ref[start + t] = piece[:2]
                bot_ref[start + t] = piece[2:]
            else:
                at = pl.ds(pl.multiple_of((start + t) * BLOCK, BLOCK), BLOCK)
                out_ref[:, at] = piece
        if gelu:
            lanes = pl.ds(pl.multiple_of(start * slab, 2 * slab), count * slab)
            harm_ref[...] += jnp.dot(
                own_ref[:, lanes], value, preferred_element_type=jnp.float32
            )

    full = blocks // GROUP

    @pl.loop(0, full)
    def _(s):
        group(s * GROUP, GROUP)

    if blocks % GROUP:
        group(full * GROUP, blocks % GROUP)


def conv_cost(blocks, channels):
    macs = blocks * BLOCK * 4 * 18 * channels * channels
    return pl.CostEstimate(flops=4 * macs, bytes_accessed=8_000_000, transcendentals=0)


def body(
    latent,
    psi_one,
    psi_two,
    cycle_one,
    cycle_two,
    w_one,
    w_two,
    b_one,
    b_two,
    lon_start,
    lon_width,
    polar_counts,
):
    row_count, col_count, channels = latent.shape
    harm_count = cycle_one.shape[3]
    lat_total = row_count * lax.axis_size("lon")
    cycle_length = col_count * lax.axis_size("lat")
    norm_factor = cycle_length ** (-0.5)
    first_row = lax.axis_index("lon") * row_count
    first_col = lax.axis_index("lat") * col_count
    east, west = shift_pairs("lat", True)
    south, north = shift_pairs("lon", False)
    out_blocks = col_count // BLOCK
    hid_blocks = out_blocks + 1
    hid_cols = hid_blocks * BLOCK

    left = lax.ppermute(latent[:, col_count - HALO :], "lat", east)
    right = lax.ppermute(latent[:, :HALO], "lat", west)
    wide = jnp.concatenate([left, latent, right], axis=1)
    up = lax.ppermute(wide[2:], "lon", south)
    down = lax.ppermute(wide[:2], "lon", north)

    own_start = lax.dynamic_slice_in_dim(lon_start, first_row, row_count, 0)
    own_width = lax.dynamic_slice_in_dim(lon_width, first_row, row_count, 0)
    taps_one = tap_matrix(psi_one, own_start, own_width, HALO - 4)
    taps_two = tap_matrix(psi_two, own_start, own_width, 0)
    columns = first_col - 2 + jnp.arange(hid_cols + 2, dtype=jnp.int32) + cycle_length
    waves = wave_rows(columns, cycle_length, harm_count)
    waves_hid, waves_out = waves[:, :hid_cols], waves[:, 2 : 2 + col_count]
    table_hid = wave_table(waves_hid, row_count)
    table_out = wave_table(waves_out, row_count)
    place = jnp.arange(hid_cols, dtype=jnp.int32)
    own = (place >= 2) & (place < 2 + col_count)
    kept = jnp.where(own[None], waves_hid, 0.0).astype(jnp.bfloat16)
    kept = kept.reshape(1, 2 * harm_count, hid_blocks, 1, BLOCK)
    eye = jnp.eye(row_count, dtype=jnp.bfloat16).reshape(row_count, 1, 1, row_count, 1)
    own_waves = (eye * kept).reshape(
        row_count * 2 * harm_count, hid_blocks * row_count * BLOCK
    )

    row_global = first_row + jnp.arange(row_count, dtype=jnp.int32)
    polar = (
        (row_global < polar_counts[0]) | (row_global >= lat_total - polar_counts[1])
    ).astype(jnp.float32)

    def cycle_mix(part, coef, w):
        lanes = row_count * 2 * harm_count
        coef_rows = coef.transpose(0, 2, 3, 1).reshape(lanes, coef.shape[1])
        polar_rows = jnp.repeat(polar, 2 * harm_count)[:, None]
        parts = lax.all_gather(part, "lat")
        return pl.pallas_call(
            functools.partial(cycle_kernel, norm_factor),
            out_shape=jax.ShapeDtypeStruct((row_count * 32, channels), jnp.bfloat16),
            compiler_params=vmem_params(),
        )(parts, coef_rows, polar_rows, w)

    part_one = jnp.einsum(
        "mj,ijc->imc",
        waves_out.astype(jnp.bfloat16),
        latent,
        preferred_element_type=jnp.float32,
    ).reshape(row_count * 2 * harm_count, channels)
    mix_one = cycle_mix(part_one, cycle_one, w_one)

    hid_half = jax.ShapeDtypeStruct((hid_blocks, 2, BLOCK, channels), jnp.bfloat16)
    feat = pltpu.VMEM((GROUP * row_count * BLOCK, w_one.shape[0]), jnp.bfloat16)

    def first_kernel(up_ref, mid_ref, dn_ref, *rest):
        conv_kernel(hid_blocks, 0, True, False, up_ref, mid_ref, None, dn_ref, *rest)

    top, bottom, part_two = pl.pallas_call(
        first_kernel,
        out_shape=(
            hid_half,
            hid_half,
            jax.ShapeDtypeStruct((row_count * 2 * harm_count, channels), jnp.float32),
        ),
        scratch_shapes=[feat],
        compiler_params=vmem_params(),
        cost_estimate=conv_cost(hid_blocks, channels),
    )(up, wide, down, taps_one, w_one, b_one[None], table_hid, mix_one, own_waves)

    hid_up = lax.ppermute(bottom, "lon", south)
    hid_down = lax.ppermute(top, "lon", north)
    mix_two = cycle_mix(part_two, cycle_two, w_two)

    def second_kernel(*refs):
        conv_kernel(out_blocks, 0, False, True, *refs)

    return pl.pallas_call(
        second_kernel,
        out_shape=jax.ShapeDtypeStruct((row_count, col_count, channels), jnp.bfloat16),
        scratch_shapes=[feat],
        compiler_params=vmem_params(),
        cost_estimate=conv_cost(out_blocks, channels),
    )(hid_up, top, bottom, hid_down, taps_two, w_two, b_two[None], table_out, mix_two)


def solution(mesh):
    return jax.shard_map(
        body,
        mesh=mesh,
        in_specs=(
            P("lon", "lat", None),
            P("lon", None, None, None),
            P("lon", None, None, None),
            P("lon", None, None, None),
            P("lon", None, None, None),
            P(),
            P(),
            P(),
            P(),
            P(),
            P(),
            P(),
        ),
        out_specs=P("lon", "lat", None),
        check_vma=False,
    )
```

```python
import functools
import math

import jax
import jax.numpy as jnp
import ml_dtypes
import numpy as np
from jax import lax
from jax.experimental import pallas as pl
from jax.experimental.pallas import tpu as pltpu
from jax.sharding import PartitionSpec as P

BLOCK = 16
EDGE = 4
TAPS = 5
FIRST_PARTS = 2
SECOND_PARTS = 3
VMEM_BYTES = 40 * 1024 * 1024
SMEM = pl.BlockSpec(memory_space=pltpu.SMEM)
VMEM = pl.BlockSpec(memory_space=pltpu.VMEM)


def vmem_params():
    return pltpu.CompilerParams(vmem_limit_bytes=VMEM_BYTES)


def wave_tables(sectors, sector_cols, rows, count):
    length = sectors * sector_cols
    cols = sector_cols + BLOCK
    first = np.array([-2, 0])[None, :, None] + sector_cols * np.arange(sectors)[:, None, None]
    place = (first + np.arange(cols)) % length
    phase = place[..., None] * np.arange(count) % length
    angles = phase * (2.0 * np.pi / length)
    waves = np.concatenate([np.cos(angles), np.sin(angles)], axis=-1).astype(np.float32)
    high = waves.astype(ml_dtypes.bfloat16).astype(np.float32)
    terms = np.concatenate([high, waves - high, high, np.zeros_like(high)], axis=-1)
    return np.tile(terms, rows).astype(ml_dtypes.bfloat16)


def taps_kernel(first, psi_ref, start_ref, width_ref, out_ref):
    rows = psi_ref.shape[0]
    width = out_ref.shape[1]
    basis = out_ref.shape[0] // (rows * BLOCK)
    first_row = lax.axis_index("lon") * rows
    source = lax.broadcasted_iota(jnp.int32, (32, TAPS * width), 0)
    lane = lax.broadcasted_iota(jnp.int32, (32, TAPS * width), 1)
    offset, height = lane // width, lane % (width // 2) // BLOCK
    r, q = source // TAPS, source % TAPS
    place_j = lax.broadcasted_iota(jnp.int32, (BLOCK, width), 0)
    place_l = lax.broadcasted_iota(jnp.int32, (BLOCK, width), 1)
    ahead = place_l // (width // 2) * BLOCK + place_l % BLOCK - place_j
    for i in range(rows):
        start, count = start_ref[first_row + i], width_ref[first_row + i]
        chosen = (r + i == height) & (start + q == offset - 2) & (q < count) & (source < TAPS * TAPS)
        chosen = jnp.where(chosen, 1.0, 0.0).astype(jnp.bfloat16)
        spread = jnp.dot(psi_ref[i], chosen, preferred_element_type=jnp.float32)
        for k in range(basis):
            taps = jnp.zeros((BLOCK, width), jnp.float32)
            for d in range(TAPS):
                row = spread[k : k + 1, d * width : (d + 1) * width]
                taps = jnp.where(ahead == first + d, row, taps)
            at = (k * rows + i) * BLOCK
            out_ref[at : at + BLOCK] = taps.astype(jnp.bfloat16)


def tap_matrix(psi, lon_start, lon_width, first):
    rows, basis = psi.shape[0], psi.shape[1]
    psi = psi.reshape(rows, basis, TAPS * TAPS)
    psi = jnp.pad(psi, ((0, 0), (0, 16 - basis), (0, 32 - TAPS * TAPS)))
    width = 2 * (rows + TAPS - 1) * BLOCK
    return pl.pallas_call(
        functools.partial(taps_kernel, first),
        out_shape=jax.ShapeDtypeStruct((basis * rows * BLOCK, width), jnp.bfloat16),
        in_specs=[VMEM, SMEM, SMEM],
        compiler_params=vmem_params(),
    )(psi, lon_start, lon_width)


def harmonic_rows(waves, row):
    part = lax.dot_general(waves, row, (((0,), (0,)), ((), ())), preferred_element_type=jnp.float32)
    return part[:8]


def packet_kernel(latent_ref, waves_ref, out_ref, edges_ref):
    rows, cols = latent_ref.shape[0], latent_ref.shape[1]
    even = lax.axis_index("lat") % 2 == 0
    waves = waves_ref[1, :cols]
    for i in range(rows):
        out_ref[8 * i : 8 * i + 8] = harmonic_rows(waves, latent_ref[i])
        left = latent_ref[i, :BLOCK].astype(jnp.float32)[:EDGE]
        right = latent_ref[i, cols - BLOCK :].astype(jnp.float32)[BLOCK - EDGE :]
        at = EDGE * i
        edges_ref[0, at : at + EDGE] = left
        edges_ref[1, at : at + EDGE] = right
        at += 8 * rows
        out_ref[at : at + EDGE] = jnp.where(even, right, left)


def sector_place():
    return lax.axis_index("lat"), lax.axis_size("lat")


def step_kernel(mask, packet_ref, got_ref, edges_ref, out_ref):
    lanes = packet_ref.shape[0] - edges_ref.shape[1]
    me, count = sector_place()
    to_right = (me ^ mask) == (me + 1) % count
    out_ref[:lanes] = packet_ref[:lanes] + got_ref[:lanes]
    out_ref[lanes:] = jnp.where(to_right, edges_ref[1], edges_ref[0])


def sides_kernel(masks, *refs):
    packet_ref, got_refs, (total_ref, upper_ref, lower_ref) = refs[0], refs[1:-3], refs[-3:]
    lanes = total_ref.shape[0]
    me, count = sector_place()
    total_ref[...] = packet_ref[:lanes] + got_refs[-1][:lanes]
    left = right = got_refs[0][lanes:]
    for mask, got_ref in zip(masks[1:], got_refs[1:]):
        left = jnp.where((me ^ mask) == (me + count - 1) % count, got_ref[lanes:], left)
        right = jnp.where((me ^ mask) == (me + 1) % count, got_ref[lanes:], right)
    blank = jnp.zeros((BLOCK - EDGE, left.shape[1]), jnp.float32)
    for i in range(4):
        own = slice(EDGE * i, EDGE * i + EDGE)
        out_ref = upper_ref if i < 2 else lower_ref
        out_ref[0, i % 2] = jnp.concatenate([blank, left[own]], axis=0).astype(jnp.bfloat16)
        out_ref[1, i % 2] = jnp.concatenate([right[own], blank], axis=0).astype(jnp.bfloat16)


def cycle_kernel(norm_factor, lat_total, total_ref, coef_ref, counts_ref, w_ref, out_ref):
    rows, basis = coef_ref.shape[0], coef_ref.shape[1]
    lanes, channels = total_ref.shape
    first_row = lax.axis_index("lon") * rows
    columns = []
    for i in range(rows):
        polar = (first_row + i < counts_ref[0]) | (first_row + i >= lat_total - counts_ref[1])
        columns.append(jnp.where(polar, coef_ref[i].T * norm_factor, 0.0))
    coefs = jnp.concatenate(columns, axis=0)
    total = total_ref[...]
    acc = jnp.zeros((2 * lanes, w_ref.shape[1]), jnp.float32)
    for k in range(basis):
        term = total * coefs[:, k : k + 1]
        high = term.astype(jnp.bfloat16)
        low = (term - high.astype(jnp.float32)).astype(jnp.bfloat16)
        acc += jnp.dot(
            jnp.concatenate([high, low], axis=0),
            w_ref[k * channels : (k + 1) * channels],
            preferred_element_type=jnp.float32,
        )
    mixed = acc[:lanes] + acc[lanes:]
    high = mixed.astype(jnp.bfloat16).astype(jnp.float32)
    low = mixed - high
    pieces = []
    for i in range(rows):
        own = slice(8 * i, 8 * i + 8)
        pieces += [high[own], high[own], low[own], jnp.zeros_like(low[own])]
    out_ref[...] = jnp.concatenate(pieces, axis=0).astype(jnp.bfloat16)


def group_values(start, count, half, taps_ref, w_ref, bias_ref, wave_block, cycle_ref, feat_ref, lift_ref):
    channels = w_ref.shape[1]
    basis = w_ref.shape[0] // channels
    slab = 4 * BLOCK
    lane = lax.broadcasted_iota(jnp.int32, (BLOCK, lift_ref.shape[1]), 1) // (lift_ref.shape[1] // 4)
    for t in range(count):
        window = jnp.concatenate([half(start, t), half(start, t + 1)], axis=0)
        feature = jnp.dot(taps_ref[...], window, preferred_element_type=jnp.float32)
        feature = feature.astype(jnp.bfloat16)
        for k in range(basis):
            feat_ref[t * slab : (t + 1) * slab, k * channels : (k + 1) * channels] = feature[
                k * slab : (k + 1) * slab
            ]
        waves = wave_block(start + t).astype(jnp.float32)
        lift = jnp.concatenate([jnp.where(lane == i, waves, 0.0) for i in range(4)], axis=0)
        lift_ref[t * slab : (t + 1) * slab] = lift.astype(jnp.bfloat16)
    size = count * slab
    mixed = jnp.dot(feat_ref[:size], w_ref[...], preferred_element_type=jnp.float32)
    mixed += jnp.dot(lift_ref[:size], cycle_ref[...], preferred_element_type=jnp.float32)
    return mixed + bias_ref[...]


def aligned(block):
    at = block * BLOCK
    return pl.ds(at if isinstance(at, int) else pl.multiple_of(at, BLOCK), BLOCK)


def first_kernel(groups, cut, up_ref, mid_ref, dn_ref, side_up_ref, side_upper_ref, side_lower_ref, side_dn_ref,
                 taps_ref, w_ref, bias_ref, waves_ref, cycle_ref,
                 top_a_ref, bot_a_ref, top_b_ref, bot_b_ref, harm_ref, feat_ref, lift_ref):
    rows, cols, channels = mid_ref.shape
    blocks = cols // BLOCK + 1

    def half(start, t):
        b = start + t
        if b in (0, blocks):
            side = 0 if b == 0 else 1
            parts = [ref[side] for ref in (side_up_ref, side_upper_ref, side_lower_ref, side_dn_ref)]
        else:
            parts = [ref[:, aligned(b - 1)] for ref in (up_ref, mid_ref, dn_ref)]
        return jnp.concatenate(parts, axis=0).reshape(8 * BLOCK, channels)

    start = 0
    for count in groups:
        mixed = group_values(start, count, half, taps_ref, w_ref, bias_ref, lambda b: waves_ref[0, aligned(b)],
                             cycle_ref, feat_ref, lift_ref)
        value = (0.5 * mixed * (1.0 + lax.erf(mixed * math.sqrt(0.5)))).astype(jnp.bfloat16)
        for t in range(count):
            b = start + t
            piece = value[t * 4 * BLOCK : (t + 1) * 4 * BLOCK].reshape(4, BLOCK, channels)
            if b <= cut:
                top_a_ref[b] = piece[:2]
                bot_a_ref[b] = piece[2:]
            if b >= cut:
                top_b_ref[b - cut] = piece[:2]
                bot_b_ref[b - cut] = piece[2:]
        start += count

    place = lax.broadcasted_iota(jnp.int32, (blocks * BLOCK, waves_ref.shape[2]), 0)
    inside = (place >= 2) & (place < 2 + cols)
    waves = jnp.where(inside, waves_ref[0].astype(jnp.float32), 0.0).astype(jnp.bfloat16)
    for i in range(rows):
        a_ref, b_ref = (top_a_ref, top_b_ref) if i < 2 else (bot_a_ref, bot_b_ref)
        row_a = a_ref[:cut, i % 2].reshape(cut * BLOCK, channels)
        row_b = b_ref[:, i % 2].reshape((blocks - cut) * BLOCK, channels)
        harm_ref[8 * i : 8 * i + 8] = harmonic_rows(waves[: cut * BLOCK], row_a) + harmonic_rows(
            waves[cut * BLOCK :], row_b
        )


def second_kernel(count, up_ref, top_ref, bot_ref, dn_ref, taps_ref, w_ref, bias_ref, waves_ref, cycle_ref, *refs):
    out_ref, feat_ref, lift_ref = refs[-3:]
    channels = top_ref.shape[3]

    def half(start, t):
        b = start + t
        parts = [ref[b] for ref in (up_ref, top_ref, bot_ref, dn_ref)]
        return jnp.concatenate(parts, axis=0).reshape(8 * BLOCK, channels)

    start = pl.program_id(0) * count
    mixed = group_values(start, count, half, taps_ref, w_ref, bias_ref,
                         lambda b: waves_ref[0, aligned(b - start)], cycle_ref, feat_ref, lift_ref)
    value = mixed.astype(jnp.bfloat16)
    for t in range(count):
        piece = value[t * 4 * BLOCK : (t + 1) * 4 * BLOCK].reshape(4, BLOCK, channels)
        out_ref[:, t * BLOCK : (t + 1) * BLOCK] = piece


def conv_cost(blocks, channels):
    macs = blocks * BLOCK * 4 * 18 * channels * channels
    return pl.CostEstimate(flops=4 * macs, bytes_accessed=8_000_000, transcendentals=0)


def swap(value, mask):
    return lax.ppermute(value, "lat", [(i, i ^ mask) for i in range(lax.axis_size("lat"))])


def body(
    latent,
    psi_one,
    psi_two,
    cycle_one,
    cycle_two,
    w_one,
    w_two,
    b_one,
    b_two,
    lon_start,
    lon_width,
    polar_counts,
):
    row_count, col_count, channels = latent.shape
    basis, harm_count = cycle_one.shape[1], cycle_one.shape[3]
    lat_total = row_count * lax.axis_size("lon")
    sectors = lax.axis_size("lat")
    norm_factor = (col_count * sectors) ** (-0.5)
    south = [(i, i + 1) for i in range(lax.axis_size("lon") - 1)]
    north = [(target, source) for source, target in south]
    out_blocks = col_count // BLOCK
    hid_blocks = out_blocks + 1
    lanes = row_count * 2 * harm_count
    masks = [2**t - 1 for t in range(1, sectors.bit_length())]
    tables = wave_tables(sectors, col_count, row_count, harm_count)
    waves = lax.dynamic_index_in_dim(jnp.asarray(tables), lax.axis_index("lat"), 0, keepdims=False)
    f32 = lambda *shape: jax.ShapeDtypeStruct(shape, jnp.float32)
    bf16 = lambda *shape: jax.ShapeDtypeStruct(shape, jnp.bfloat16)

    edge_rows = row_count * EDGE
    packet, edges = pl.pallas_call(
        packet_kernel,
        out_shape=(f32(lanes + edge_rows, channels), f32(2, edge_rows, channels)),
        compiler_params=vmem_params(),
    )(latent, waves)
    up = lax.ppermute(latent[2:], "lon", south)
    down = lax.ppermute(latent[:2], "lon", north)
    gots = [swap(packet, masks[0])]
    for mask in masks[1:]:
        packet = pl.pallas_call(
            functools.partial(step_kernel, mask),
            out_shape=f32(*packet.shape),
            compiler_params=vmem_params(),
        )(packet, gots[-1], edges)
        gots.append(swap(packet, mask))
    side = bf16(2, 2, BLOCK, channels)
    total_one, side_upper, side_lower = pl.pallas_call(
        functools.partial(sides_kernel, masks),
        out_shape=(f32(lanes, channels), side, side),
        compiler_params=vmem_params(),
    )(packet, *gots)
    side_up = lax.ppermute(side_lower, "lon", south)
    side_down = lax.ppermute(side_upper, "lon", north)

    def cycle_mix(total, cycle, w):
        return pl.pallas_call(
            functools.partial(cycle_kernel, norm_factor, lat_total),
            out_shape=bf16(row_count * 32, channels),
            in_specs=[VMEM, VMEM, SMEM, VMEM],
            compiler_params=vmem_params(),
        )(total, cycle.reshape(row_count, basis, 2 * harm_count), polar_counts, w)

    def scratch(count):
        size = count * row_count * BLOCK
        return [
            pltpu.VMEM((size, basis * channels), jnp.bfloat16),
            pltpu.VMEM((size, row_count * 32), jnp.bfloat16),
        ]

    taps_one = tap_matrix(psi_one, lon_start, lon_width, BLOCK - EDGE)
    mix_one = cycle_mix(total_one, cycle_one, w_one)
    part = -(-hid_blocks // FIRST_PARTS)
    groups = [min(part, hid_blocks - at) for at in range(0, hid_blocks, part)]
    tail = out_blocks // SECOND_PARTS
    cut = out_blocks - tail
    hid_a = bf16(cut + 1, 2, BLOCK, channels)
    hid_b = bf16(hid_blocks - cut, 2, BLOCK, channels)
    top_a, bot_a, top_b, bot_b, part_two = pl.pallas_call(
        functools.partial(first_kernel, groups, cut),
        out_shape=(hid_a, hid_a, hid_b, hid_b, f32(lanes, channels)),
        scratch_shapes=scratch(part),
        compiler_params=vmem_params(),
        cost_estimate=conv_cost(hid_blocks, channels),
    )(up, latent, down, side_up, side_upper, side_lower, side_down, taps_one, w_one, b_one[None], waves, mix_one)

    up_a = lax.ppermute(bot_a, "lon", south)
    down_a = lax.ppermute(top_a, "lon", north)
    up_b = lax.ppermute(bot_b, "lon", south)
    down_b = lax.ppermute(top_b, "lon", north)
    total_two = part_two
    for mask in masks:
        total_two = total_two + swap(total_two, mask)
    psi_two, _ = lax.optimization_barrier((psi_two, part_two))
    taps_two = tap_matrix(psi_two, lon_start, lon_width, 0)
    mix_two = cycle_mix(total_two, cycle_two, w_two)

    def second(first, steps, sources, result):
        count = tail
        whole = lambda value: pl.BlockSpec(value.shape, lambda s: (0,) * value.ndim)
        operands = list(sources) + [taps_two, w_two, b_two[None], waves, mix_two]
        in_specs = [whole(value) for value in operands]
        in_specs[-2] = pl.BlockSpec((1, count * BLOCK, waves.shape[2]), lambda s: (1, first + s, 0))
        aliases = {}
        if result is not None:
            aliases = {len(operands): 0}
            operands.append(result)
            in_specs.append(pl.BlockSpec(memory_space=pl.ANY))
        return pl.pallas_call(
            functools.partial(second_kernel, count),
            grid=(steps,),
            out_shape=bf16(row_count, col_count, channels),
            in_specs=in_specs,
            out_specs=pl.BlockSpec((row_count, count * BLOCK, channels), lambda s: (0, first + s, 0)),
            input_output_aliases=aliases,
            scratch_shapes=scratch(count),
            compiler_params=vmem_params(),
            cost_estimate=conv_cost(count * steps, channels),
        )(*operands)

    steps = SECOND_PARTS - 1
    result = second(0, steps, (up_a, top_a, bot_a, down_a), None)
    return second(steps, 1, (up_b, top_b, bot_b, down_b), result)


def solution(mesh):
    return jax.shard_map(
        body,
        mesh=mesh,
        in_specs=(
            P("lon", "lat", None),
            P("lon", None, None, None),
            P("lon", None, None, None),
            P("lon", None, None, None),
            P("lon", None, None, None),
            P(),
            P(),
            P(),
            P(),
            P(),
            P(),
            P(),
        ),
        out_specs=P("lon", "lat", None),
        check_vma=False,
    )
```

```python
import functools
import math

import jax
import jax.numpy as jnp
import ml_dtypes
import numpy as np
from jax import lax
from jax.experimental import pallas as pl
from jax.experimental.pallas import tpu as pltpu
from jax.sharding import PartitionSpec as P

BLOCK = 16
EDGE = 4
TAPS = 5
VMEM_BYTES = 40 * 1024 * 1024
SMALL_BYTES = 16 * 1024 * 1024
SMEM = pl.BlockSpec(memory_space=pltpu.SMEM)
VMEM = pl.BlockSpec(memory_space=pltpu.VMEM)
HBM = pl.BlockSpec(memory_space=pltpu.HBM)
LITTLE = pl.CostEstimate(flops=1, bytes_accessed=1, transcendentals=0)


def vmem_params(size=SMALL_BYTES):
    return pltpu.CompilerParams(vmem_limit_bytes=size)


def wave_tables(sectors, sector_cols, rows, count):
    length = sectors * sector_cols
    cols = sector_cols + BLOCK
    first = np.array([-2, 0])[None, :, None] + sector_cols * np.arange(sectors)[:, None, None]
    place = (first + np.arange(cols)) % length
    phase = place[..., None] * np.arange(count) % length
    angles = phase * (2.0 * np.pi / length)
    waves = np.concatenate([np.cos(angles), np.sin(angles)], axis=-1).astype(np.float32)
    high = waves.astype(ml_dtypes.bfloat16).astype(np.float32)
    terms = np.concatenate([high, waves - high, high, np.zeros_like(high)], axis=-1)
    lanes = np.tile(terms, rows).astype(ml_dtypes.bfloat16)
    across = high[:, 1, :sector_cols].transpose(0, 2, 1)
    across = np.concatenate([across, np.zeros_like(across)], axis=1).astype(ml_dtypes.bfloat16)
    return jnp.asarray(lanes), jnp.asarray(across)


def band_pairs(count):
    pairs = []
    for first in (0, 1):
        south = [(i, i + 1) for i in range(first, count - 1, 2)]
        pairs.append(south + [(target, source) for source, target in south])
    return pairs


def exchange(payloads):
    pairs = band_pairs(lax.axis_size("lon"))
    return [lax.ppermute(value, "lon", pair) for value, pair in zip(payloads, pairs)]


def first_is_south():
    return lax.axis_index("lon") % 2 == 0


def payloads(upper, lower):
    south = first_is_south()
    return jnp.where(south, lower, upper), jnp.where(south, upper, lower)


def start_copies(pairs, sems):
    copies = [pltpu.make_async_copy(source, target, sems.at[n]) for n, (source, target) in enumerate(pairs)]
    for copy in copies:
        copy.start()
    return copies


def taps_kernel(first, sent, psi_ref, start_ref, width_ref, out_ref):
    rows = psi_ref.shape[0]
    width = out_ref.shape[1]
    basis = out_ref.shape[0] // (rows * BLOCK)
    first_row = lax.axis_index("lon") * rows
    source = lax.broadcasted_iota(jnp.int32, (32, TAPS * width), 0)
    lane = lax.broadcasted_iota(jnp.int32, (32, TAPS * width), 1)
    offset, height = lane // width, lane % (width // 2) // BLOCK
    swapped = 6 - height // 2 * 2 + height % 2
    if not sent:
        swapped = jnp.where((height < 2) | (height >= 6), swapped, height)
    height = jnp.where(first_is_south(), swapped, height)
    r, q = source // TAPS, source % TAPS
    place_j = lax.broadcasted_iota(jnp.int32, (BLOCK, width), 0)
    place_l = lax.broadcasted_iota(jnp.int32, (BLOCK, width), 1)
    ahead = place_l // (width // 2) * BLOCK + place_l % BLOCK - place_j
    for i in range(rows):
        start, count = start_ref[first_row + i], width_ref[first_row + i]
        chosen = (r + i == height) & (start + q == offset - 2) & (q < count) & (source < TAPS * TAPS)
        chosen = jnp.where(chosen, 1.0, 0.0).astype(jnp.bfloat16)
        spread = jnp.dot(psi_ref[i], chosen, preferred_element_type=jnp.float32)
        for k in range(basis):
            taps = jnp.zeros((BLOCK, width), jnp.float32)
            for d in range(TAPS):
                row = spread[k : k + 1, d * width : (d + 1) * width]
                taps = jnp.where(ahead == first + d, row, taps)
            at = (k * rows + i) * BLOCK
            out_ref[at : at + BLOCK] = taps.astype(jnp.bfloat16)


def tap_matrix(psi, lon_start, lon_width, first, sent):
    rows, basis = psi.shape[0], psi.shape[1]
    psi = psi.reshape(rows, basis, TAPS * TAPS)
    psi = jnp.pad(psi, ((0, 0), (0, 16 - basis), (0, 32 - TAPS * TAPS)))
    width = 2 * (rows + TAPS - 1) * BLOCK
    return pl.pallas_call(
        functools.partial(taps_kernel, first, sent),
        out_shape=jax.ShapeDtypeStruct((basis * rows * BLOCK, width), jnp.bfloat16),
        in_specs=[VMEM, SMEM, SMEM],
        cost_estimate=LITTLE,
        compiler_params=vmem_params(),
    )(psi, lon_start, lon_width)


def harmonic_rows(waves, row):
    part = lax.dot_general(waves, row, (((0,), (0,)), ((), ())), preferred_element_type=jnp.float32)
    return part[:8]


def packet_kernel(latent_ref, across_ref, out_ref, edges_ref, one_ref, two_ref, out_sems):
    rows, cols = latent_ref.shape[0], latent_ref.shape[1]
    even = lax.axis_index("lat") % 2 == 0
    first = jnp.where(first_is_south(), 2, 0)
    payload = [(latent_ref.at[pl.ds(at, 2)], ref) for at, ref in ((first, one_ref), (2 - first, two_ref))]
    sends = start_copies(payload, out_sems)
    across = across_ref[lax.axis_index("lat")]
    for i in range(rows):
        part = jnp.dot(across, latent_ref[i], preferred_element_type=jnp.float32)
        out_ref[8 * i : 8 * i + 8] = part[:8]
        left = latent_ref[i, :BLOCK].astype(jnp.float32)[:EDGE]
        right = latent_ref[i, cols - BLOCK :].astype(jnp.float32)[BLOCK - EDGE :]
        at = EDGE * i
        edges_ref[0, at : at + EDGE] = left
        edges_ref[1, at : at + EDGE] = right
        at += 8 * rows
        out_ref[at : at + EDGE] = jnp.where(even, right, left)
    for copy in sends:
        copy.wait()


def sector_place():
    return lax.axis_index("lat"), lax.axis_size("lat")


def step_kernel(mask, packet_ref, got_ref, edges_ref, out_ref):
    lanes = packet_ref.shape[0] - edges_ref.shape[1]
    me, count = sector_place()
    to_right = (me ^ mask) == (me + 1) % count
    out_ref[:lanes] = packet_ref[:lanes] + got_ref[:lanes]
    out_ref[lanes:] = jnp.where(to_right, edges_ref[1], edges_ref[0])


def sides_kernel(masks, *refs):
    packet_ref, got_refs, (total_ref, upper_ref, lower_ref, one_ref, two_ref) = refs[0], refs[1:-5], refs[-5:]
    lanes = total_ref.shape[0]
    me, count = sector_place()
    total_ref[...] = packet_ref[:lanes] + got_refs[-1][:lanes]
    left = right = got_refs[0][lanes:]
    for mask, got_ref in zip(masks[1:], got_refs[1:]):
        left = jnp.where((me ^ mask) == (me + count - 1) % count, got_ref[lanes:], left)
        right = jnp.where((me ^ mask) == (me + 1) % count, got_ref[lanes:], right)
    blank = jnp.zeros((BLOCK - EDGE, left.shape[1]), jnp.float32)
    for i in range(4):
        own = slice(EDGE * i, EDGE * i + EDGE)
        out_ref = upper_ref if i < 2 else lower_ref
        out_ref[0, i % 2] = jnp.concatenate([blank, left[own]], axis=0).astype(jnp.bfloat16)
        out_ref[1, i % 2] = jnp.concatenate([right[own], blank], axis=0).astype(jnp.bfloat16)
    one_ref[...], two_ref[...] = payloads(upper_ref[...], lower_ref[...])


def cycle_mix(norm_factor, lat_total, total_ref, coef_ref, counts_ref, w_ref):
    rows, basis = coef_ref.shape[0], coef_ref.shape[1]
    lanes, channels = total_ref.shape
    first_row = lax.axis_index("lon") * rows
    columns = []
    for i in range(rows):
        polar = (first_row + i < counts_ref[0]) | (first_row + i >= lat_total - counts_ref[1])
        columns.append(jnp.where(polar, coef_ref[i].T * norm_factor, 0.0))
    coefs = jnp.concatenate(columns, axis=0)
    total = total_ref[...]
    acc = jnp.zeros((2 * lanes, w_ref.shape[1]), jnp.float32)
    for k in range(basis):
        term = total * coefs[:, k : k + 1]
        high = term.astype(jnp.bfloat16)
        low = (term - high.astype(jnp.float32)).astype(jnp.bfloat16)
        acc += jnp.dot(
            jnp.concatenate([high, low], axis=0),
            w_ref[k * channels : (k + 1) * channels],
            preferred_element_type=jnp.float32,
        )
    mixed = acc[:lanes] + acc[lanes:]
    high = mixed.astype(jnp.bfloat16).astype(jnp.float32)
    low = mixed - high
    pieces = []
    for i in range(rows):
        own = slice(8 * i, 8 * i + 8)
        pieces += [high[own], high[own], low[own], jnp.zeros_like(low[own])]
    return jnp.concatenate(pieces, axis=0).astype(jnp.bfloat16)


def group_values(start, count, half, taps_ref, w_ref, bias_ref, wave_block, cycle_ref, feat_ref, lift_ref):
    channels = w_ref.shape[1]
    basis = w_ref.shape[0] // channels
    slab = 4 * BLOCK
    lane = lax.broadcasted_iota(jnp.int32, (BLOCK, lift_ref.shape[1]), 1) // (lift_ref.shape[1] // 4)
    for t in range(count):
        window = jnp.concatenate([half(start, t), half(start, t + 1)], axis=0)
        feature = jnp.dot(taps_ref[...], window, preferred_element_type=jnp.float32)
        feature = feature.astype(jnp.bfloat16)
        for k in range(basis):
            feat_ref[t * slab : (t + 1) * slab, k * channels : (k + 1) * channels] = feature[
                k * slab : (k + 1) * slab
            ]
        waves = wave_block(start + t).astype(jnp.float32)
        lift = jnp.concatenate([jnp.where(lane == i, waves, 0.0) for i in range(4)], axis=0)
        lift_ref[t * slab : (t + 1) * slab] = lift.astype(jnp.bfloat16)
    size = count * slab
    mixed = jnp.dot(feat_ref[:size], w_ref[...], preferred_element_type=jnp.float32)
    mixed += jnp.dot(lift_ref[:size], cycle_ref[...], preferred_element_type=jnp.float32)
    return mixed + bias_ref[...]


def aligned(block):
    at = block * BLOCK
    return pl.ds(at if isinstance(at, int) else pl.multiple_of(at, BLOCK), BLOCK)


def first_kernel(mix, first, count, one_hbm, two_hbm, mid_ref, waves_ref, w_ref, side_one_ref, side_upper_ref,
                 side_lower_ref, side_two_ref, taps_ref, bias_ref, *refs):
    feat_ref, lift_ref, one_ref, two_ref, sems = refs[-5:]
    if first:
        before_ref, cycle_ref, pay_one_ref, pay_two_ref, harm_ref = refs[:-5]
    else:
        total_ref, coef_ref, counts_ref, pay_one_ref, pay_two_ref, harm_ref, cycle_ref = refs[:-5]
    rows, cols, channels = mid_ref.shape
    blocks = cols // BLOCK + 1
    low = max(first - 1, 0)
    own = pl.ds(low * BLOCK, one_ref.shape[1])
    copies = start_copies([(one_hbm.at[:, own], one_ref), (two_hbm.at[:, own], two_ref)], sems)
    if not first:
        cycle_ref[...] = mix(total_ref, coef_ref, counts_ref, w_ref)

    def half(start, t):
        b = start + t
        if b in (0, blocks):
            side = 0 if b == 0 else 1
            parts = [ref[side] for ref in (side_one_ref, side_upper_ref, side_lower_ref, side_two_ref)]
        else:
            at = aligned(b - 1 - low)
            parts = [one_ref[:, at], mid_ref[:, aligned(b - 1)], two_ref[:, at]]
        return jnp.concatenate(parts, axis=0).reshape(8 * BLOCK, channels)

    for copy in copies:
        copy.wait()
    mixed = group_values(first, count, half, taps_ref, w_ref, bias_ref,
                         lambda b: waves_ref[0, aligned(b)], cycle_ref, feat_ref, lift_ref)
    value = (0.5 * mixed * (1.0 + lax.erf(mixed * math.sqrt(0.5)))).astype(jnp.bfloat16)
    for t in range(count):
        piece = value[t * 4 * BLOCK : (t + 1) * 4 * BLOCK].reshape(4, BLOCK, channels)
        pay_one_ref[t], pay_two_ref[t] = payloads(piece[:2], piece[2:])

    size = count * BLOCK
    place = lax.broadcasted_iota(jnp.int32, (size, waves_ref.shape[2]), 0) + first * BLOCK
    inside = (place >= 2) & (place < 2 + cols)
    waves = waves_ref[0, first * BLOCK : first * BLOCK + size].astype(jnp.float32)
    waves = jnp.where(inside, waves, 0.0).astype(jnp.bfloat16)
    parts = [
        jnp.concatenate([harmonic_rows(waves, ref[:, r].reshape(size, channels)) for r in range(2)], axis=0)
        for ref in (pay_one_ref, pay_two_ref)
    ]
    total = jnp.concatenate(payloads(*parts), axis=0)
    if first:
        total += before_ref[...]
    harm_ref[...] = total


def second_kernel(mix, groups, *refs):
    parts = [refs[at : at + 4] for at in range(0, 4 * len(groups), 4)]
    refs = refs[4 * len(groups) :]
    total_ref, coef_ref, counts_ref, waves_ref, w_ref, taps_ref, bias_ref, out_hbm, feat_ref, lift_ref, cycle_ref = refs[:11]
    refs = refs[11:]
    out_refs, out_sems = refs[:-1], refs[-1]
    channels = w_ref.shape[1]
    cycle_ref[...] = mix(total_ref, coef_ref, counts_ref, w_ref)
    place = [(part, at) for part in range(len(groups)) for at in range(parts[part][0].shape[0])]

    def half(start, t):
        part, at = place[start + t]
        return jnp.concatenate([ref[at] for ref in parts[part]], axis=0).reshape(8 * BLOCK, channels)

    start, sends = 0, []
    for n, (count, out_ref) in enumerate(zip(groups, out_refs)):
        mixed = group_values(start, count, half, taps_ref, w_ref, bias_ref, lambda b: waves_ref[1, aligned(b)],
                             cycle_ref, feat_ref, lift_ref)
        value = mixed.astype(jnp.bfloat16)
        for t in range(count):
            out_ref[:, aligned(t)] = value[t * 4 * BLOCK : (t + 1) * 4 * BLOCK].reshape(4, BLOCK, channels)
        at = pl.ds(start * BLOCK, count * BLOCK)
        send = pltpu.make_async_copy(out_ref, out_hbm.at[:, at], out_sems.at[n])
        send.start()
        sends.append(send)
        start += count
    for send in sends:
        send.wait()


def conv_cost(blocks, channels):
    macs = blocks * BLOCK * 4 * 18 * channels * channels
    return pl.CostEstimate(flops=4 * macs, bytes_accessed=8_000_000, transcendentals=0)


def swap(value, mask):
    return lax.ppermute(value, "lat", [(i, i ^ mask) for i in range(lax.axis_size("lat"))])


def body(
    latent,
    psi_one,
    psi_two,
    cycle_one,
    cycle_two,
    w_one,
    w_two,
    b_one,
    b_two,
    lon_start,
    lon_width,
    polar_counts,
):
    row_count, col_count, channels = latent.shape
    basis, harm_count = cycle_one.shape[1], cycle_one.shape[3]
    lat_total = row_count * lax.axis_size("lon")
    sectors = lax.axis_size("lat")
    norm_factor = (col_count * sectors) ** (-0.5)
    out_blocks = col_count // BLOCK
    hid_blocks = out_blocks + 1
    lanes = row_count * 2 * harm_count
    masks = [2**t - 1 for t in range(1, sectors.bit_length())]
    tables, across = wave_tables(sectors, col_count, row_count, harm_count)
    waves = lax.dynamic_index_in_dim(tables, lax.axis_index("lat"), 0, keepdims=False)
    f32 = lambda *shape: jax.ShapeDtypeStruct(shape, jnp.float32)
    bf16 = lambda *shape: jax.ShapeDtypeStruct(shape, jnp.bfloat16)
    held = lambda *shape: pltpu.VMEM(shape, jnp.bfloat16)
    sems = lambda count: pltpu.SemaphoreType.DMA((count,))

    edge_rows = row_count * EDGE
    rows_shape = bf16(2, col_count, channels)
    packet, edges, *rows = pl.pallas_call(
        packet_kernel,
        out_shape=(f32(lanes + edge_rows, channels), f32(2, edge_rows, channels), rows_shape, rows_shape),
        in_specs=[VMEM, VMEM],
        out_specs=[VMEM, VMEM, HBM, HBM],
        scratch_shapes=[sems(2)],
        cost_estimate=LITTLE,
        compiler_params=vmem_params(),
    )(latent, across)
    row_one, row_two = exchange(rows)
    gots = [swap(packet, masks[0])]
    for mask in masks[1:]:
        packet = pl.pallas_call(
            functools.partial(step_kernel, mask),
            cost_estimate=LITTLE,
            out_shape=f32(*packet.shape),
            compiler_params=vmem_params(),
        )(packet, gots[-1], edges)
        gots.append(swap(packet, mask))
    side = bf16(2, 2, BLOCK, channels)
    total_one, side_upper, side_lower, *sides = pl.pallas_call(
        functools.partial(sides_kernel, masks),
        cost_estimate=LITTLE,
        out_shape=(f32(lanes, channels), side, side, side, side),
        compiler_params=vmem_params(),
    )(packet, *gots)
    side_one, side_two = exchange(sides)

    mix = functools.partial(cycle_mix, norm_factor, lat_total)
    mix_shape = (row_count * 32, channels)
    coefs = lambda cycle: cycle.reshape(row_count, basis, 2 * harm_count)

    def scratch(count):
        size = count * row_count * BLOCK
        return [held(size, basis * channels), held(size, mix_shape[0])]

    taps_one = tap_matrix(psi_one, lon_start, lon_width, BLOCK - EDGE, False)
    cut = hid_blocks // 2
    hidden = []
    for first, count in ((0, cut), (cut, hid_blocks - cut)):
        operands = (row_one, row_two, latent, waves, w_one, side_one, side_upper, side_lower, side_two, taps_one)
        operands += (b_one[None],)
        half = bf16(count, 2, BLOCK, channels)
        out_shape = (half, half, f32(lanes, channels))
        in_specs = [HBM] * 2 + [VMEM] * (len(operands) - 2)
        if first:
            operands += (harmonics, mix_one)
            in_specs += [VMEM, VMEM]
        else:
            operands += (total_one, coefs(cycle_one), polar_counts)
            in_specs += [VMEM, VMEM, SMEM]
            out_shape += (bf16(*mix_shape),)
        own = (min(first + count, out_blocks) - max(first - 1, 0)) * BLOCK
        pay_one, pay_two, harmonics, *made = pl.pallas_call(
            functools.partial(first_kernel, mix, first, count),
            out_shape=out_shape,
            in_specs=in_specs,
            scratch_shapes=scratch(count) + [held(2, own, channels), held(2, own, channels), sems(2)],
            compiler_params=vmem_params(VMEM_BYTES),
            cost_estimate=LITTLE,
        )(*operands)
        mix_one = made[0] if made else mix_one
        got_one, got_two = exchange((pay_one, pay_two))
        hidden += [got_one, pay_one, pay_two, got_two]

    total_two = harmonics + swap(harmonics, masks[0])
    for got in (hidden[0], hidden[3]):
        total_two += 0.0 * got[0, 0, :1].astype(jnp.float32)
    for mask in masks[1:]:
        total_two = total_two + swap(total_two, mask)
    psi_two, _ = lax.optimization_barrier((psi_two, harmonics))
    taps_two = tap_matrix(psi_two, lon_start, lon_width, 0, True)
    groups = (cut, out_blocks - cut)
    operands = (*hidden, total_two, coefs(cycle_two), polar_counts, waves, w_two, taps_two, b_two[None])
    return pl.pallas_call(
        functools.partial(second_kernel, mix, groups),
        out_shape=bf16(row_count, col_count, channels),
        in_specs=[VMEM] * (len(hidden) + 2) + [SMEM] + [VMEM] * 4,
        out_specs=HBM,
        scratch_shapes=scratch(max(groups))
        + [held(*mix_shape)]
        + [held(row_count, count * BLOCK, channels) for count in groups]
        + [sems(len(groups))],
        compiler_params=vmem_params(56 * 1024 * 1024),
        cost_estimate=conv_cost(out_blocks, channels),
    )(*operands)


def solution(mesh):
    return jax.shard_map(
        body,
        mesh=mesh,
        in_specs=(
            P("lon", "lat", None),
            P("lon", None, None, None),
            P("lon", None, None, None),
            P("lon", None, None, None),
            P("lon", None, None, None),
            P(),
            P(),
            P(),
            P(),
            P(),
            P(),
            P(),
        ),
        out_specs=P("lon", "lat", None),
        check_vma=False,
    )
```

```python
import functools
import math

import jax
import jax.numpy as jnp
import ml_dtypes
import numpy as np
from jax import lax
from jax.experimental import pallas as pl
from jax.experimental.pallas import tpu as pltpu
from jax.sharding import PartitionSpec as P

BLOCK = 16
EDGE = 4
TAPS = 5
VMEM_BYTES = 40 * 1024 * 1024
SMALL_BYTES = 16 * 1024 * 1024
SMEM = pl.BlockSpec(memory_space=pltpu.SMEM)
VMEM = pl.BlockSpec(memory_space=pltpu.VMEM)
HBM = pl.BlockSpec(memory_space=pltpu.HBM)
LITTLE = pl.CostEstimate(flops=1, bytes_accessed=1, transcendentals=0)


def vmem_params(size=SMALL_BYTES):
    return pltpu.CompilerParams(vmem_limit_bytes=size)


def wave_tables(sectors, sector_cols, rows, count):
    length = sectors * sector_cols
    cols = sector_cols + BLOCK
    first = np.array([-2, 0])[None, :, None] + sector_cols * np.arange(sectors)[:, None, None]
    place = (first + np.arange(cols)) % length
    phase = place[..., None] * np.arange(count) % length
    angles = phase * (2.0 * np.pi / length)
    waves = np.concatenate([np.cos(angles), np.sin(angles)], axis=-1).astype(np.float32)
    high = waves.astype(ml_dtypes.bfloat16).astype(np.float32)
    terms = np.concatenate([high, waves - high, high, np.zeros_like(high)], axis=-1)
    lanes = np.tile(terms, rows).astype(ml_dtypes.bfloat16)
    return jnp.asarray(lanes)


def band_pairs(count):
    pairs = []
    for first in (0, 1):
        south = [(i, i + 1) for i in range(first, count - 1, 2)]
        pairs.append(south + [(target, source) for source, target in south])
    return pairs


def exchange(payloads):
    pairs = band_pairs(lax.axis_size("lon"))
    return [lax.ppermute(value, "lon", pair) for value, pair in zip(payloads, pairs)]


def first_is_south():
    return lax.axis_index("lon") % 2 == 0


def payloads(upper, lower):
    south = first_is_south()
    return jnp.where(south, lower, upper), jnp.where(south, upper, lower)


def start_copies(pairs, sems):
    copies = [pltpu.make_async_copy(source, target, sems.at[n]) for n, (source, target) in enumerate(pairs)]
    for copy in copies:
        copy.start()
    return copies


def taps_kernel(first, sent, psi_ref, start_ref, width_ref, out_ref):
    rows = psi_ref.shape[0]
    width = out_ref.shape[1]
    basis = out_ref.shape[0] // (rows * BLOCK)
    first_row = lax.axis_index("lon") * rows
    source = lax.broadcasted_iota(jnp.int32, (32, TAPS * width), 0)
    lane = lax.broadcasted_iota(jnp.int32, (32, TAPS * width), 1)
    offset, height = lane // width, lane % (width // 2) // BLOCK
    swapped = 6 - height // 2 * 2 + height % 2
    if not sent:
        swapped = jnp.where((height < 2) | (height >= 6), swapped, height)
    height = jnp.where(first_is_south(), swapped, height)
    r, q = source // TAPS, source % TAPS
    place_j = lax.broadcasted_iota(jnp.int32, (BLOCK, width), 0)
    place_l = lax.broadcasted_iota(jnp.int32, (BLOCK, width), 1)
    ahead = place_l // (width // 2) * BLOCK + place_l % BLOCK - place_j
    for i in range(rows):
        start, count = start_ref[first_row + i], width_ref[first_row + i]
        chosen = (r + i == height) & (start + q == offset - 2) & (q < count) & (source < TAPS * TAPS)
        chosen = jnp.where(chosen, 1.0, 0.0).astype(jnp.bfloat16)
        spread = jnp.dot(psi_ref[i], chosen, preferred_element_type=jnp.float32)
        for k in range(basis):
            taps = jnp.zeros((BLOCK, width), jnp.float32)
            for d in range(TAPS):
                row = spread[k : k + 1, d * width : (d + 1) * width]
                taps = jnp.where(ahead == first + d, row, taps)
            at = (k * rows + i) * BLOCK
            out_ref[at : at + BLOCK] = taps.astype(jnp.bfloat16)


def tap_matrices(psis, lon_start, lon_width, layers):
    rows, basis = psis[0].shape[0], psis[0].shape[1]

    def kernel(*refs):
        psi_refs, (start_ref, width_ref), out_refs = refs[: len(layers)], refs[len(layers) : -len(layers)], refs[-len(layers) :]
        for (first, sent), psi_ref, out_ref in zip(layers, psi_refs, out_refs):
            taps_kernel(first, sent, psi_ref, start_ref, width_ref, out_ref)

    psis = [psi.reshape(rows, basis, TAPS * TAPS) for psi in psis]
    psis = [jnp.pad(psi, ((0, 0), (0, 16 - basis), (0, 32 - TAPS * TAPS))) for psi in psis]
    shape = jax.ShapeDtypeStruct((basis * rows * BLOCK, 2 * (rows + TAPS - 1) * BLOCK), jnp.bfloat16)
    return pl.pallas_call(
        kernel,
        out_shape=[shape] * len(layers),
        in_specs=[VMEM] * len(layers) + [SMEM, SMEM],
        cost_estimate=LITTLE,
        compiler_params=vmem_params(),
    )(*psis, lon_start, lon_width)


def harmonic_rows(waves, row):
    part = lax.dot_general(waves, row, (((0,), (0,)), ((), ())), preferred_element_type=jnp.float32)
    return part[:8]


def packet_kernel(count, latent_ref, out_ref, edges_ref, one_ref, two_ref, out_sems):
    rows, cols = latent_ref.shape[0], latent_ref.shape[1]
    even = lax.axis_index("lat") % 2 == 0
    first = jnp.where(first_is_south(), 2, 0)
    payload = [(latent_ref.at[pl.ds(at, 2)], ref) for at, ref in ((first, one_ref), (2 - first, two_ref))]
    sends = start_copies(payload, out_sems)
    length = cols * lax.axis_size("lat")
    column = lax.axis_index("lat") * cols + lax.broadcasted_iota(jnp.int32, (count, cols), 1)
    phase = column * lax.broadcasted_iota(jnp.int32, (count, cols), 0) % length
    angles = phase.astype(jnp.float32) * jnp.float32(2.0 * math.pi / length)
    blank = jnp.zeros((16 - 2 * count, cols), jnp.float32)
    across = jnp.concatenate([jnp.cos(angles), jnp.sin(angles), blank], axis=0).astype(jnp.bfloat16)
    for i in range(rows):
        part = jnp.dot(across, latent_ref[i], preferred_element_type=jnp.float32)
        out_ref[8 * i : 8 * i + 8] = part[:8]
        left = latent_ref[i, :BLOCK].astype(jnp.float32)[:EDGE]
        right = latent_ref[i, cols - BLOCK :].astype(jnp.float32)[BLOCK - EDGE :]
        at = EDGE * i
        edges_ref[0, at : at + EDGE] = left
        edges_ref[1, at : at + EDGE] = right
        at += 8 * rows
        out_ref[at : at + EDGE] = jnp.where(even, right, left)
    for copy in sends:
        copy.wait()


def sector_place():
    return lax.axis_index("lat"), lax.axis_size("lat")


def step_kernel(mask, packet_ref, got_ref, edges_ref, out_ref):
    lanes = packet_ref.shape[0] - edges_ref.shape[1]
    me, count = sector_place()
    to_right = (me ^ mask) == (me + 1) % count
    out_ref[:lanes] = packet_ref[:lanes] + got_ref[:lanes]
    out_ref[lanes:] = jnp.where(to_right, edges_ref[1], edges_ref[0])


def sides_kernel(masks, *refs):
    packet_ref, got_refs, (total_ref, upper_ref, lower_ref, one_ref, two_ref) = refs[0], refs[1:-5], refs[-5:]
    lanes = total_ref.shape[0]
    me, count = sector_place()
    total_ref[...] = packet_ref[:lanes] + got_refs[-1][:lanes]
    left = right = got_refs[0][lanes:]
    for mask, got_ref in zip(masks[1:], got_refs[1:]):
        left = jnp.where((me ^ mask) == (me + count - 1) % count, got_ref[lanes:], left)
        right = jnp.where((me ^ mask) == (me + 1) % count, got_ref[lanes:], right)
    blank = jnp.zeros((BLOCK - EDGE, left.shape[1]), jnp.float32)
    for i in range(4):
        own = slice(EDGE * i, EDGE * i + EDGE)
        out_ref = upper_ref if i < 2 else lower_ref
        out_ref[0, i % 2] = jnp.concatenate([blank, left[own]], axis=0).astype(jnp.bfloat16)
        out_ref[1, i % 2] = jnp.concatenate([right[own], blank], axis=0).astype(jnp.bfloat16)
    one_ref[...], two_ref[...] = payloads(upper_ref[...], lower_ref[...])


def cycle_mix(norm_factor, lat_total, layer, total, coef_ref, counts_ref, w_ref):
    rows, basis = coef_ref.shape[1], coef_ref.shape[2]
    lanes, channels = total.shape
    first_row = lax.axis_index("lon") * rows
    columns = []
    for i in range(rows):
        polar = (first_row + i < counts_ref[0]) | (first_row + i >= lat_total - counts_ref[1])
        columns.append(jnp.where(polar, coef_ref[layer, i].T * norm_factor, 0.0))
    coefs = jnp.concatenate(columns, axis=0)
    acc = jnp.zeros((2 * lanes, w_ref.shape[1]), jnp.float32)
    for k in range(basis):
        term = total * coefs[:, k : k + 1]
        high = term.astype(jnp.bfloat16)
        low = (term - high.astype(jnp.float32)).astype(jnp.bfloat16)
        acc += jnp.dot(
            jnp.concatenate([high, low], axis=0),
            w_ref[k * channels : (k + 1) * channels],
            preferred_element_type=jnp.float32,
        )
    mixed = acc[:lanes] + acc[lanes:]
    high = mixed.astype(jnp.bfloat16).astype(jnp.float32)
    low = mixed - high
    pieces = []
    for i in range(rows):
        own = slice(8 * i, 8 * i + 8)
        pieces += [high[own], high[own], low[own], jnp.zeros_like(low[own])]
    return jnp.concatenate(pieces, axis=0).astype(jnp.bfloat16)


def group_values(start, count, half, taps_ref, w_ref, bias_ref, wave_block, cycle_ref, feat_ref, lift_ref):
    channels = w_ref.shape[1]
    basis = w_ref.shape[0] // channels
    slab = 4 * BLOCK
    lane = lax.broadcasted_iota(jnp.int32, (BLOCK, lift_ref.shape[1]), 1) // (lift_ref.shape[1] // 4)
    for t in range(count):
        window = jnp.concatenate([half(start, t), half(start, t + 1)], axis=0)
        feature = jnp.dot(taps_ref[...], window, preferred_element_type=jnp.float32)
        feature = feature.astype(jnp.bfloat16)
        for k in range(basis):
            feat_ref[t * slab : (t + 1) * slab, k * channels : (k + 1) * channels] = feature[
                k * slab : (k + 1) * slab
            ]
        waves = wave_block(start + t).astype(jnp.float32)
        lift = jnp.concatenate([jnp.where(lane == i, waves, 0.0) for i in range(4)], axis=0)
        lift_ref[t * slab : (t + 1) * slab] = lift.astype(jnp.bfloat16)
    size = count * slab
    mixed = jnp.dot(feat_ref[:size], w_ref[...], preferred_element_type=jnp.float32)
    mixed += jnp.dot(lift_ref[:size], cycle_ref[...], preferred_element_type=jnp.float32)
    return mixed + bias_ref[...]


def aligned(block):
    at = block * BLOCK
    return pl.ds(at if isinstance(at, int) else pl.multiple_of(at, BLOCK), BLOCK)


def first_kernel(mix, first, count, one_hbm, two_hbm, mid_ref, waves_ref, w_ref, side_one_ref, side_upper_ref,
                 side_lower_ref, side_two_ref, taps_ref, bias_ref, *refs):
    feat_ref, lift_ref, one_ref, two_ref, sems = refs[-5:]
    if first:
        before_ref, cycle_ref, pay_one_ref, pay_two_ref, harm_ref = refs[:-5]
    else:
        total_ref, coef_ref, counts_ref, pay_one_ref, pay_two_ref, harm_ref, cycle_ref = refs[:-5]
    rows, cols, channels = mid_ref.shape
    blocks = cols // BLOCK + 1
    low = max(first - 1, 0)
    own = pl.ds(low * BLOCK, one_ref.shape[1])
    copies = start_copies([(one_hbm.at[:, own], one_ref), (two_hbm.at[:, own], two_ref)], sems)
    if not first:
        cycle_ref[...] = mix(0, total_ref[...], coef_ref, counts_ref, w_ref)

    def half(start, t):
        b = start + t
        if b in (0, blocks):
            side = 0 if b == 0 else 1
            parts = [ref[side] for ref in (side_one_ref, side_upper_ref, side_lower_ref, side_two_ref)]
        else:
            at = aligned(b - 1 - low)
            parts = [one_ref[:, at], mid_ref[:, aligned(b - 1)], two_ref[:, at]]
        return jnp.concatenate(parts, axis=0).reshape(8 * BLOCK, channels)

    for copy in copies:
        copy.wait()
    mixed = group_values(first, count, half, taps_ref, w_ref, bias_ref,
                         lambda b: waves_ref[0, aligned(b)], cycle_ref, feat_ref, lift_ref)
    value = (0.5 * mixed * (1.0 + lax.erf(mixed * math.sqrt(0.5)))).astype(jnp.bfloat16)
    for t in range(count):
        piece = value[t * 4 * BLOCK : (t + 1) * 4 * BLOCK].reshape(4, BLOCK, channels)
        pay_one_ref[t], pay_two_ref[t] = payloads(piece[:2], piece[2:])

    size = count * BLOCK
    place = lax.broadcasted_iota(jnp.int32, (size, waves_ref.shape[2]), 0) + first * BLOCK
    inside = (place >= 2) & (place < 2 + cols)
    waves = waves_ref[0, first * BLOCK : first * BLOCK + size].astype(jnp.float32)
    waves = jnp.where(inside, waves, 0.0).astype(jnp.bfloat16)
    parts = [
        jnp.concatenate([harmonic_rows(waves, ref[:, r].reshape(size, channels)) for r in range(2)], axis=0)
        for ref in (pay_one_ref, pay_two_ref)
    ]
    total = jnp.concatenate(payloads(*parts), axis=0)
    if first:
        total += before_ref[...]
    harm_ref[...] = total


def second_kernel(mix, groups, *refs):
    parts = [refs[at : at + 4] for at in range(0, 4 * len(groups), 4)]
    refs = refs[4 * len(groups) :]
    total_ref, rest_ref, coef_ref, counts_ref, waves_ref, w_ref, taps_ref, bias_ref, out_hbm, *refs = refs
    feat_ref, lift_ref, cycle_ref, *refs = refs
    out_refs, out_sems = refs[:-1], refs[-1]
    channels = w_ref.shape[1]
    cycle_ref[...] = mix(1, total_ref[...] + rest_ref[...], coef_ref, counts_ref, w_ref)
    place = [(part, at) for part in range(len(groups)) for at in range(parts[part][0].shape[0])]

    def half(start, t):
        part, at = place[start + t]
        return jnp.concatenate([ref[at] for ref in parts[part]], axis=0).reshape(8 * BLOCK, channels)

    start, sends = 0, []
    for n, (count, out_ref) in enumerate(zip(groups, out_refs)):
        mixed = group_values(start, count, half, taps_ref, w_ref, bias_ref, lambda b: waves_ref[1, aligned(b)],
                             cycle_ref, feat_ref, lift_ref)
        value = mixed.astype(jnp.bfloat16)
        for t in range(count):
            out_ref[:, aligned(t)] = value[t * 4 * BLOCK : (t + 1) * 4 * BLOCK].reshape(4, BLOCK, channels)
        at = pl.ds(start * BLOCK, count * BLOCK)
        send = pltpu.make_async_copy(out_ref, out_hbm.at[:, at], out_sems.at[n])
        send.start()
        sends.append(send)
        start += count
    for send in sends:
        send.wait()


def conv_cost(blocks, channels):
    macs = blocks * BLOCK * 4 * 18 * channels * channels
    return pl.CostEstimate(flops=4 * macs, bytes_accessed=8_000_000, transcendentals=0)


def swap(value, mask):
    return lax.ppermute(value, "lat", [(i, i ^ mask) for i in range(lax.axis_size("lat"))])


def body(
    latent,
    psi_one,
    psi_two,
    cycle_one,
    cycle_two,
    w_one,
    w_two,
    b_one,
    b_two,
    lon_start,
    lon_width,
    polar_counts,
):
    row_count, col_count, channels = latent.shape
    basis, harm_count = cycle_one.shape[1], cycle_one.shape[3]
    lat_total = row_count * lax.axis_size("lon")
    sectors = lax.axis_size("lat")
    norm_factor = (col_count * sectors) ** (-0.5)
    out_blocks = col_count // BLOCK
    hid_blocks = out_blocks + 1
    lanes = row_count * 2 * harm_count
    masks = [2**t - 1 for t in range(1, sectors.bit_length())]
    tables = wave_tables(sectors, col_count, row_count, harm_count)
    waves = lax.dynamic_index_in_dim(tables, lax.axis_index("lat"), 0, keepdims=False)
    f32 = lambda *shape: jax.ShapeDtypeStruct(shape, jnp.float32)
    bf16 = lambda *shape: jax.ShapeDtypeStruct(shape, jnp.bfloat16)
    held = lambda *shape: pltpu.VMEM(shape, jnp.bfloat16)
    sems = lambda count: pltpu.SemaphoreType.DMA((count,))

    edge_rows = row_count * EDGE
    rows_shape = bf16(2, col_count, channels)
    packet, edges, *rows = pl.pallas_call(
        functools.partial(packet_kernel, harm_count),
        out_shape=(f32(lanes + edge_rows, channels), f32(2, edge_rows, channels), rows_shape, rows_shape),
        out_specs=[VMEM, VMEM, HBM, HBM],
        scratch_shapes=[sems(2)],
        cost_estimate=LITTLE,
        compiler_params=vmem_params(),
    )(latent)
    row_one, row_two = exchange(rows)
    gots = [swap(packet, masks[0])]
    for mask in masks[1:]:
        packet = pl.pallas_call(
            functools.partial(step_kernel, mask),
            cost_estimate=LITTLE,
            out_shape=f32(*packet.shape),
            compiler_params=vmem_params(),
        )(packet, gots[-1], edges)
        gots.append(swap(packet, mask))
    side = bf16(2, 2, BLOCK, channels)
    total_one, side_upper, side_lower, *sides = pl.pallas_call(
        functools.partial(sides_kernel, masks),
        cost_estimate=LITTLE,
        out_shape=(f32(lanes, channels), side, side, side, side),
        compiler_params=vmem_params(),
    )(packet, *gots)
    side_one, side_two = exchange(sides)

    mix = functools.partial(cycle_mix, norm_factor, lat_total)
    mix_shape = (row_count * 32, channels)
    coefs = jnp.stack([cycle_one, cycle_two]).reshape(2, row_count, basis, 2 * harm_count)

    def scratch(count):
        size = count * row_count * BLOCK
        return [held(size, basis * channels), held(size, mix_shape[0])]

    taps_one, taps_two = tap_matrices(
        (psi_one, psi_two), lon_start, lon_width, ((BLOCK - EDGE, False), (0, True))
    )
    cut = hid_blocks * 28 // 46
    hidden = []
    for first, count in ((0, cut), (cut, hid_blocks - cut)):
        operands = (row_one, row_two, latent, waves, w_one, side_one, side_upper, side_lower, side_two, taps_one)
        operands += (b_one[None],)
        half = bf16(count, 2, BLOCK, channels)
        out_shape = (half, half, f32(lanes, channels))
        in_specs = [HBM] * 2 + [VMEM] * (len(operands) - 2)
        if first:
            operands += (harmonics, mix_one)
            in_specs += [VMEM, VMEM]
        else:
            operands += (total_one, coefs, polar_counts)
            in_specs += [VMEM, VMEM, SMEM]
            out_shape += (bf16(*mix_shape),)
        own = (min(first + count, out_blocks) - max(first - 1, 0)) * BLOCK
        pay_one, pay_two, harmonics, *made = pl.pallas_call(
            functools.partial(first_kernel, mix, first, count),
            out_shape=out_shape,
            in_specs=in_specs,
            scratch_shapes=scratch(count) + [held(2, own, channels), held(2, own, channels), sems(2)],
            compiler_params=vmem_params(VMEM_BYTES),
            cost_estimate=LITTLE,
        )(*operands)
        mix_one = made[0] if made else mix_one
        got_one, got_two = exchange((pay_one, pay_two))
        hidden += [got_one, pay_one, pay_two, got_two]

    hops = [2**t for t in range(sectors.bit_length() - 1)]
    total_two = harmonics + swap(harmonics, hops[0])
    for hop in hops[1:-1]:
        total_two = total_two + swap(total_two, hop)
    for got in (hidden[0], hidden[3]):
        total_two += 0.0 * got[0, 0, :1].astype(jnp.float32)
    rest_two = swap(total_two, hops[-1])
    groups = (cut, out_blocks - cut)
    operands = (*hidden, total_two, rest_two, coefs, polar_counts, waves, w_two, taps_two, b_two[None])
    return pl.pallas_call(
        functools.partial(second_kernel, mix, groups),
        out_shape=bf16(row_count, col_count, channels),
        in_specs=[VMEM] * (len(hidden) + 3) + [SMEM] + [VMEM] * 4,
        out_specs=HBM,
        scratch_shapes=scratch(max(groups))
        + [held(*mix_shape)]
        + [held(row_count, count * BLOCK, channels) for count in groups]
        + [sems(len(groups))],
        compiler_params=vmem_params(56 * 1024 * 1024),
        cost_estimate=conv_cost(out_blocks, channels),
    )(*operands)


def solution(mesh):
    return jax.shard_map(
        body,
        mesh=mesh,
        in_specs=(
            P("lon", "lat", None),
            P("lon", None, None, None),
            P("lon", None, None, None),
            P("lon", None, None, None),
            P("lon", None, None, None),
            P(),
            P(),
            P(),
            P(),
            P(),
            P(),
            P(),
        ),
        out_specs=P("lon", "lat", None),
        check_vma=False,
    )
```

```python
import functools
import math

import jax
import jax.numpy as jnp
import ml_dtypes
import numpy as np
from jax import lax
from jax.experimental import pallas as pl
from jax.experimental.pallas import tpu as pltpu
from jax.sharding import PartitionSpec as P

BLOCK = 16
EDGE = 4
TAPS = 5
VMEM_BYTES = 40 * 1024 * 1024
SMALL_BYTES = 16 * 1024 * 1024
SMEM = pl.BlockSpec(memory_space=pltpu.SMEM)
VMEM = pl.BlockSpec(memory_space=pltpu.VMEM)
HBM = pl.BlockSpec(memory_space=pltpu.HBM)
LITTLE = pl.CostEstimate(flops=1, bytes_accessed=1, transcendentals=0)


def vmem_params(size=SMALL_BYTES):
    return pltpu.CompilerParams(vmem_limit_bytes=size)


def wave_tables(sectors, sector_cols, rows, count):
    length = sectors * sector_cols
    cols = sector_cols + BLOCK
    first = np.array([-2, 0])[None, :, None] + sector_cols * np.arange(sectors)[:, None, None]
    place = (first + np.arange(cols)) % length
    phase = place[..., None] * np.arange(count) % length
    angles = phase * (2.0 * np.pi / length)
    waves = np.concatenate([np.cos(angles), np.sin(angles)], axis=-1).astype(np.float32)
    high = waves.astype(ml_dtypes.bfloat16).astype(np.float32)
    terms = np.concatenate([high, waves - high, high, np.zeros_like(high)], axis=-1)
    lanes = np.tile(terms, rows).astype(ml_dtypes.bfloat16)
    return jnp.asarray(lanes)


def band_pairs(count):
    pairs = []
    for first in (0, 1):
        south = [(i, i + 1) for i in range(first, count - 1, 2)]
        pairs.append(south + [(target, source) for source, target in south])
    return pairs


def exchange(payloads):
    pairs = band_pairs(lax.axis_size("lon"))
    return [lax.ppermute(value, "lon", pair) for value, pair in zip(payloads, pairs)]


def first_is_south():
    return lax.axis_index("lon") % 2 == 0


def payloads(upper, lower):
    south = first_is_south()
    return jnp.where(south, lower, upper), jnp.where(south, upper, lower)


def start_copies(pairs, sems):
    copies = [pltpu.make_async_copy(source, target, sems.at[n]) for n, (source, target) in enumerate(pairs)]
    for copy in copies:
        copy.start()
    return copies


def taps_kernel(first, sent, psi_ref, start_ref, width_ref, out_ref):
    rows = psi_ref.shape[0]
    width = out_ref.shape[1]
    basis = out_ref.shape[0] // (rows * BLOCK)
    first_row = lax.axis_index("lon") * rows
    source = lax.broadcasted_iota(jnp.int32, (32, TAPS * width), 0)
    lane = lax.broadcasted_iota(jnp.int32, (32, TAPS * width), 1)
    offset, height = lane // width, lane % (width // 2) // BLOCK
    swapped = 6 - height // 2 * 2 + height % 2
    if not sent:
        swapped = jnp.where((height < 2) | (height >= 6), swapped, height)
    height = jnp.where(first_is_south(), swapped, height)
    r, q = source // TAPS, source % TAPS
    place_j = lax.broadcasted_iota(jnp.int32, (BLOCK, width), 0)
    place_l = lax.broadcasted_iota(jnp.int32, (BLOCK, width), 1)
    ahead = place_l // (width // 2) * BLOCK + place_l % BLOCK - place_j
    for i in range(rows):
        start, count = start_ref[first_row + i], width_ref[first_row + i]
        chosen = (r + i == height) & (start + q == offset - 2) & (q < count) & (source < TAPS * TAPS)
        chosen = jnp.where(chosen, 1.0, 0.0).astype(jnp.bfloat16)
        spread = jnp.dot(psi_ref[i], chosen, preferred_element_type=jnp.float32)
        for k in range(basis):
            taps = jnp.zeros((BLOCK, width), jnp.float32)
            for d in range(TAPS):
                row = spread[k : k + 1, d * width : (d + 1) * width]
                taps = jnp.where(ahead == first + d, row, taps)
            at = (k * rows + i) * BLOCK
            out_ref[at : at + BLOCK] = taps.astype(jnp.bfloat16)


def tap_matrices(psis, lon_start, lon_width, layers):
    rows, basis = psis[0].shape[0], psis[0].shape[1]

    def kernel(*refs):
        psi_refs, (start_ref, width_ref), out_refs = refs[: len(layers)], refs[len(layers) : -len(layers)], refs[-len(layers) :]
        for (first, sent), psi_ref, out_ref in zip(layers, psi_refs, out_refs):
            taps_kernel(first, sent, psi_ref, start_ref, width_ref, out_ref)

    psis = [psi.reshape(rows, basis, TAPS * TAPS) for psi in psis]
    psis = [jnp.pad(psi, ((0, 0), (0, 16 - basis), (0, 32 - TAPS * TAPS))) for psi in psis]
    shape = jax.ShapeDtypeStruct((basis * rows * BLOCK, 2 * (rows + TAPS - 1) * BLOCK), jnp.bfloat16)
    return pl.pallas_call(
        kernel,
        out_shape=[shape] * len(layers),
        in_specs=[VMEM] * len(layers) + [SMEM, SMEM],
        cost_estimate=LITTLE,
        compiler_params=vmem_params(),
    )(*psis, lon_start, lon_width)


def harmonic_rows(waves, row):
    part = lax.dot_general(waves, row, (((0,), (0,)), ((), ())), preferred_element_type=jnp.float32)
    return part[:8]


def packet_kernel(count, latent_ref, out_ref, edges_ref, one_ref, two_ref, out_sems):
    rows, cols = latent_ref.shape[0], latent_ref.shape[1]
    even = lax.axis_index("lat") % 2 == 0
    first = jnp.where(first_is_south(), 2, 0)
    payload = [(latent_ref.at[pl.ds(at, 2)], ref) for at, ref in ((first, one_ref), (2 - first, two_ref))]
    sends = start_copies(payload, out_sems)
    length = cols * lax.axis_size("lat")
    column = lax.axis_index("lat") * cols + lax.broadcasted_iota(jnp.int32, (count, cols), 1)
    phase = column * lax.broadcasted_iota(jnp.int32, (count, cols), 0) % length
    angles = phase.astype(jnp.float32) * jnp.float32(2.0 * math.pi / length)
    blank = jnp.zeros((16 - 2 * count, cols), jnp.float32)
    across = jnp.concatenate([jnp.cos(angles), jnp.sin(angles), blank], axis=0).astype(jnp.bfloat16)
    for i in range(rows):
        part = jnp.dot(across, latent_ref[i], preferred_element_type=jnp.float32)
        out_ref[8 * i : 8 * i + 8] = part[:8]
        left = latent_ref[i, :BLOCK].astype(jnp.float32)[:EDGE]
        right = latent_ref[i, cols - BLOCK :].astype(jnp.float32)[BLOCK - EDGE :]
        at = EDGE * i
        edges_ref[0, at : at + EDGE] = left
        edges_ref[1, at : at + EDGE] = right
        at += 8 * rows
        out_ref[at : at + EDGE] = jnp.where(even, right, left)
    for copy in sends:
        copy.wait()


def sector_place():
    return lax.axis_index("lat"), lax.axis_size("lat")


def step_kernel(mask, packet_ref, got_ref, edges_ref, out_ref):
    lanes = packet_ref.shape[0] - edges_ref.shape[1]
    me, count = sector_place()
    to_right = (me ^ mask) == (me + 1) % count
    out_ref[:lanes] = packet_ref[:lanes] + got_ref[:lanes]
    out_ref[lanes:] = jnp.where(to_right, edges_ref[1], edges_ref[0])


def sides_kernel(masks, *refs):
    packet_ref, got_refs, (total_ref, upper_ref, lower_ref, one_ref, two_ref) = refs[0], refs[1:-5], refs[-5:]
    lanes = total_ref.shape[0]
    me, count = sector_place()
    total_ref[...] = packet_ref[:lanes] + got_refs[-1][:lanes]
    left = right = got_refs[0][lanes:]
    for mask, got_ref in zip(masks[1:], got_refs[1:]):
        left = jnp.where((me ^ mask) == (me + count - 1) % count, got_ref[lanes:], left)
        right = jnp.where((me ^ mask) == (me + 1) % count, got_ref[lanes:], right)
    blank = jnp.zeros((BLOCK - EDGE, left.shape[1]), jnp.float32)
    for i in range(4):
        own = slice(EDGE * i, EDGE * i + EDGE)
        out_ref = upper_ref if i < 2 else lower_ref
        out_ref[0, i % 2] = jnp.concatenate([blank, left[own]], axis=0).astype(jnp.bfloat16)
        out_ref[1, i % 2] = jnp.concatenate([right[own], blank], axis=0).astype(jnp.bfloat16)
    one_ref[...], two_ref[...] = payloads(upper_ref[...], lower_ref[...])


def cycle_mix(norm_factor, lat_total, layer, total, coef_ref, counts_ref, w_ref):
    rows, basis = coef_ref.shape[1], coef_ref.shape[2]
    lanes, channels = total.shape
    first_row = lax.axis_index("lon") * rows
    columns = []
    for i in range(rows):
        polar = (first_row + i < counts_ref[0]) | (first_row + i >= lat_total - counts_ref[1])
        columns.append(jnp.where(polar, coef_ref[layer, i].T * norm_factor, 0.0))
    coefs = jnp.concatenate(columns, axis=0)
    acc = jnp.zeros((2 * lanes, w_ref.shape[1]), jnp.float32)
    for k in range(basis):
        term = total * coefs[:, k : k + 1]
        high = term.astype(jnp.bfloat16)
        low = (term - high.astype(jnp.float32)).astype(jnp.bfloat16)
        acc += jnp.dot(
            jnp.concatenate([high, low], axis=0),
            w_ref[k * channels : (k + 1) * channels],
            preferred_element_type=jnp.float32,
        )
    mixed = acc[:lanes] + acc[lanes:]
    high = mixed.astype(jnp.bfloat16).astype(jnp.float32)
    low = mixed - high
    pieces = []
    for i in range(rows):
        own = slice(8 * i, 8 * i + 8)
        pieces += [high[own], high[own], low[own], jnp.zeros_like(low[own])]
    return jnp.concatenate(pieces, axis=0).astype(jnp.bfloat16)


def group_values(start, count, half, taps_ref, w_ref, bias_ref, wave_block, cycle_ref, feat_ref, lift_ref):
    channels = w_ref.shape[1]
    basis = w_ref.shape[0] // channels
    slab = 4 * BLOCK
    lane = lax.broadcasted_iota(jnp.int32, (BLOCK, lift_ref.shape[1]), 1) // (lift_ref.shape[1] // 4)
    for t in range(count):
        window = jnp.concatenate([half(start, t), half(start, t + 1)], axis=0)
        feature = jnp.dot(taps_ref[...], window, preferred_element_type=jnp.float32)
        feature = feature.astype(jnp.bfloat16)
        for k in range(basis):
            feat_ref[t * slab : (t + 1) * slab, k * channels : (k + 1) * channels] = feature[
                k * slab : (k + 1) * slab
            ]
        waves = wave_block(start + t).astype(jnp.float32)
        lift = jnp.concatenate([jnp.where(lane == i, waves, 0.0) for i in range(4)], axis=0)
        lift_ref[t * slab : (t + 1) * slab] = lift.astype(jnp.bfloat16)
    size = count * slab
    mixed = jnp.dot(feat_ref[:size], w_ref[...], preferred_element_type=jnp.float32)
    mixed += jnp.dot(lift_ref[:size], cycle_ref[...], preferred_element_type=jnp.float32)
    return mixed + bias_ref[...]


def aligned(block):
    at = block * BLOCK
    return pl.ds(at if isinstance(at, int) else pl.multiple_of(at, BLOCK), BLOCK)


def first_kernel(mix, first, count, pieces, one_hbm, two_hbm, mid_ref, waves_ref, w_ref, side_one_ref, side_upper_ref,
                 side_lower_ref, side_two_ref, taps_ref, bias_ref, *refs):
    feat_ref, lift_ref, one_ref, two_ref, sems = refs[-5:]
    if first:
        before_ref, cycle_ref, pay_one_ref, pay_two_ref, harm_ref = refs[:-5]
    else:
        total_ref, coef_ref, counts_ref, pay_one_ref, pay_two_ref, harm_ref, cycle_ref = refs[:-5]
    rows, cols, channels = mid_ref.shape
    blocks = cols // BLOCK + 1
    low = max(first - 1, 0)
    own = pl.ds(low * BLOCK, one_ref.shape[1])
    copies = start_copies([(one_hbm.at[:, own], one_ref), (two_hbm.at[:, own], two_ref)], sems)
    if not first:
        cycle_ref[...] = mix(0, total_ref[...], coef_ref, counts_ref, w_ref)

    def half(start, t):
        b = start + t
        if b in (0, blocks):
            side = 0 if b == 0 else 1
            parts = [ref[side] for ref in (side_one_ref, side_upper_ref, side_lower_ref, side_two_ref)]
        else:
            at = aligned(b - 1 - low)
            parts = [one_ref[:, at], mid_ref[:, aligned(b - 1)], two_ref[:, at]]
        return jnp.concatenate(parts, axis=0).reshape(8 * BLOCK, channels)

    for copy in copies:
        copy.wait()
    start = 0
    for size in split(count, pieces):
        mixed = group_values(first + start, size, half, taps_ref, w_ref, bias_ref,
                             lambda b: waves_ref[0, aligned(b)], cycle_ref, feat_ref, lift_ref)
        value = (0.5 * mixed * (1.0 + lax.erf(mixed * math.sqrt(0.5)))).astype(jnp.bfloat16)
        for t in range(size):
            piece = value[t * 4 * BLOCK : (t + 1) * 4 * BLOCK].reshape(4, BLOCK, channels)
            pay_one_ref[start + t], pay_two_ref[start + t] = payloads(piece[:2], piece[2:])
        start += size

    size = count * BLOCK
    place = lax.broadcasted_iota(jnp.int32, (size, waves_ref.shape[2]), 0) + first * BLOCK
    inside = (place >= 2) & (place < 2 + cols)
    waves = waves_ref[0, first * BLOCK : first * BLOCK + size].astype(jnp.float32)
    waves = jnp.where(inside, waves, 0.0).astype(jnp.bfloat16)
    parts = [
        jnp.concatenate([harmonic_rows(waves, ref[:, r].reshape(size, channels)) for r in range(2)], axis=0)
        for ref in (pay_one_ref, pay_two_ref)
    ]
    total = jnp.concatenate(payloads(*parts), axis=0)
    if first:
        total += before_ref[...]
    harm_ref[...] = total


def second_kernel(mix, groups, *refs):
    parts = [refs[:4], refs[4:8]]
    refs = refs[8:]
    total_ref, rest_ref, coef_ref, counts_ref, waves_ref, w_ref, taps_ref, bias_ref, out_hbm, *refs = refs
    feat_ref, lift_ref, cycle_ref, *refs = refs
    out_refs, out_sems = refs[:-1], refs[-1]
    channels = w_ref.shape[1]
    cycle_ref[...] = mix(1, total_ref[...] + rest_ref[...], coef_ref, counts_ref, w_ref)
    place = [(part, at) for part in range(len(parts)) for at in range(parts[part][0].shape[0])]

    def half(start, t):
        part, at = place[start + t]
        return jnp.concatenate([ref[at] for ref in parts[part]], axis=0).reshape(8 * BLOCK, channels)

    start, sends = 0, []
    for n, (count, out_ref) in enumerate(zip(groups, out_refs)):
        mixed = group_values(start, count, half, taps_ref, w_ref, bias_ref, lambda b: waves_ref[1, aligned(b)],
                             cycle_ref, feat_ref, lift_ref)
        value = mixed.astype(jnp.bfloat16)
        for t in range(count):
            out_ref[:, aligned(t)] = value[t * 4 * BLOCK : (t + 1) * 4 * BLOCK].reshape(4, BLOCK, channels)
        at = pl.ds(start * BLOCK, count * BLOCK)
        send = pltpu.make_async_copy(out_ref, out_hbm.at[:, at], out_sems.at[n])
        send.start()
        sends.append(send)
        start += count
    for send in sends:
        send.wait()


def conv_cost(blocks, channels):
    macs = blocks * BLOCK * 4 * 18 * channels * channels
    return pl.CostEstimate(flops=4 * macs, bytes_accessed=8_000_000, transcendentals=0)


def split(count, pieces):
    return [count * (n + 1) // pieces - count * n // pieces for n in range(pieces)]


def swap(value, mask):
    return lax.ppermute(value, "lat", [(i, i ^ mask) for i in range(lax.axis_size("lat"))])


def body(
    latent,
    psi_one,
    psi_two,
    cycle_one,
    cycle_two,
    w_one,
    w_two,
    b_one,
    b_two,
    lon_start,
    lon_width,
    polar_counts,
):
    row_count, col_count, channels = latent.shape
    basis, harm_count = cycle_one.shape[1], cycle_one.shape[3]
    lat_total = row_count * lax.axis_size("lon")
    sectors = lax.axis_size("lat")
    norm_factor = (col_count * sectors) ** (-0.5)
    out_blocks = col_count // BLOCK
    hid_blocks = out_blocks + 1
    lanes = row_count * 2 * harm_count
    masks = [2**t - 1 for t in range(1, sectors.bit_length())]
    tables = wave_tables(sectors, col_count, row_count, harm_count)
    waves = lax.dynamic_index_in_dim(tables, lax.axis_index("lat"), 0, keepdims=False)
    f32 = lambda *shape: jax.ShapeDtypeStruct(shape, jnp.float32)
    bf16 = lambda *shape: jax.ShapeDtypeStruct(shape, jnp.bfloat16)
    held = lambda *shape: pltpu.VMEM(shape, jnp.bfloat16)
    sems = lambda count: pltpu.SemaphoreType.DMA((count,))

    edge_rows = row_count * EDGE
    rows_shape = bf16(2, col_count, channels)
    packet, edges, *rows = pl.pallas_call(
        functools.partial(packet_kernel, harm_count),
        out_shape=(f32(lanes + edge_rows, channels), f32(2, edge_rows, channels), rows_shape, rows_shape),
        out_specs=[VMEM, VMEM, HBM, HBM],
        scratch_shapes=[sems(2)],
        cost_estimate=LITTLE,
        compiler_params=vmem_params(),
    )(latent)
    row_one, row_two = exchange(rows)
    gots = [swap(packet, masks[0])]
    for mask in masks[1:]:
        packet = pl.pallas_call(
            functools.partial(step_kernel, mask),
            cost_estimate=LITTLE,
            out_shape=f32(*packet.shape),
            compiler_params=vmem_params(),
        )(packet, gots[-1], edges)
        gots.append(swap(packet, mask))
    side = bf16(2, 2, BLOCK, channels)
    total_one, side_upper, side_lower, *sides = pl.pallas_call(
        functools.partial(sides_kernel, masks),
        cost_estimate=LITTLE,
        out_shape=(f32(lanes, channels), side, side, side, side),
        compiler_params=vmem_params(),
    )(packet, *gots)
    side_one, side_two = exchange(sides)

    mix = functools.partial(cycle_mix, norm_factor, lat_total)
    mix_shape = (row_count * 32, channels)
    coefs = jnp.stack([cycle_one, cycle_two]).reshape(2, row_count, basis, 2 * harm_count)

    def scratch(count):
        size = count * row_count * BLOCK
        return [held(size, basis * channels), held(size, mix_shape[0])]

    taps_one, taps_two = tap_matrices(
        (psi_one, psi_two), lon_start, lon_width, ((BLOCK - EDGE, False), (0, True))
    )
    cut = hid_blocks * 30 // 46
    hidden = []
    for first, count, pieces in ((0, cut, 2), (cut, hid_blocks - cut, 1)):
        operands = (row_one, row_two, latent, waves, w_one, side_one, side_upper, side_lower, side_two, taps_one)
        operands += (b_one[None],)
        half = bf16(count, 2, BLOCK, channels)
        out_shape = (half, half, f32(lanes, channels))
        in_specs = [HBM] * 2 + [VMEM] * (len(operands) - 2)
        if first:
            operands += (harmonics, mix_one)
            in_specs += [VMEM, VMEM]
        else:
            operands += (total_one, coefs, polar_counts)
            in_specs += [VMEM, VMEM, SMEM]
            out_shape += (bf16(*mix_shape),)
        own = (min(first + count, out_blocks) - max(first - 1, 0)) * BLOCK
        pay_one, pay_two, harmonics, *made = pl.pallas_call(
            functools.partial(first_kernel, mix, first, count, pieces),
            out_shape=out_shape,
            in_specs=in_specs,
            scratch_shapes=scratch(count) + [held(2, own, channels), held(2, own, channels), sems(2)],
            compiler_params=vmem_params(VMEM_BYTES),
            cost_estimate=LITTLE,
        )(*operands)
        mix_one = made[0] if made else mix_one
        got_one, got_two = exchange((pay_one, pay_two))
        hidden += [got_one, pay_one, pay_two, got_two]

    hops = [2**t for t in range(sectors.bit_length() - 1)]
    total_two = harmonics + swap(harmonics, hops[0])
    for hop in hops[1:-1]:
        total_two = total_two + swap(total_two, hop)
    for got in (hidden[0], hidden[3]):
        total_two += 0.0 * got[0, 0, :1].astype(jnp.float32)
    rest_two = swap(total_two, hops[-1])
    groups = split(out_blocks, 3)
    operands = (*hidden, total_two, rest_two, coefs, polar_counts, waves, w_two, taps_two, b_two[None])
    return pl.pallas_call(
        functools.partial(second_kernel, mix, groups),
        out_shape=bf16(row_count, col_count, channels),
        in_specs=[VMEM] * (len(hidden) + 3) + [SMEM] + [VMEM] * 4,
        out_specs=HBM,
        scratch_shapes=scratch(max(groups))
        + [held(*mix_shape)]
        + [held(row_count, count * BLOCK, channels) for count in groups]
        + [sems(len(groups))],
        compiler_params=vmem_params(56 * 1024 * 1024),
        cost_estimate=conv_cost(out_blocks, channels),
    )(*operands)


def solution(mesh):
    return jax.shard_map(
        body,
        mesh=mesh,
        in_specs=(
            P("lon", "lat", None),
            P("lon", None, None, None),
            P("lon", None, None, None),
            P("lon", None, None, None),
            P("lon", None, None, None),
            P(),
            P(),
            P(),
            P(),
            P(),
            P(),
            P(),
        ),
        out_specs=P("lon", "lat", None),
        check_vma=False,
    )
```
